32 devices in a mesh: dp: 4 (over y, x), ctx: 2 (over core), head: 4 (over z).
Axes of the slice: x: 2, y: 2, z: 4, core: 2. Of those that a mesh axis runs over, the one named last changes fastest.
Arguments:
- queries: bfloat16 [4, 1024, 2048], P('dp', 'ctx', 'head'), may hold values from -6 to 6
- keys: bfloat16 [4, 1024, 2048], P('dp', 'ctx', 'head'), may hold values from -6 to 6
- values: bfloat16 [4, 1024, 2048], P('dp', 'ctx', 'head'), may hold values from -6 to 6
- decay: float32 [4, 16, 1024], P('dp', 'head', 'ctx'), may hold values from 0.4 to 1
- beta: float32 [4, 16, 1024], P('dp', 'head', 'ctx'), may hold values from 0 to 1
- inputs: bfloat16 [4, 1024, 4096], P('dp', 'ctx'), may hold values from -6 to 6
- probe: bfloat16 [4096, 2048], P(('dp', 'ctx'), 'head'), may hold values from -0.09375 to 0.09375
Outputs:
- mixed: bfloat16 [4, 1024, 2048], P('dp', 'ctx', 'head')
- curvature: float32 [4096, 2048], P(('dp', 'ctx'), 'head')
The draws below stay inside these ranges and needn't reach their ends.
All inputs are finite; a program needn't handle non-finite values.
Results may differ from the reference program's by a relative error of at most 0.006.
Values may be sent and summed in bfloat16 or wider, within the bound.
No kernel may reach another device: no remote copies, remote signals or barrier semaphores. Data moves between devices by JAX's collectives and lax.ppermute only.
A program may use at most 128 MiB of HBM per device.

```python
import math
import jax
import jax.numpy as jnp
from jax import lax

D = 4096
ATTENTION_UNITS = 16
DK = 128
TOK_DEV = 512
SAMPLE_TOTAL = 4
TOKEN_SPAN = 1024


def slow_heads(key, share):
    picks = jax.random.randint(key, (SAMPLE_TOTAL, ATTENTION_UNITS, 1), 0, 1000)
    return picks < share


def draw_decay(key, part):
    share = 500
    slow_mask = slow_heads(key, share)
    key = jax.random.fold_in(key, 11)
    derived_generator_seeds = jax.random.split(key, 6)
    fast_rate = jnp.exp(jax.random.uniform(derived_generator_seeds[0], (SAMPLE_TOTAL, ATTENTION_UNITS, 1), jnp.float32, math.log(1.0 / 50.0), math.log(1.0 / 30.0)))
    slow_rate = jnp.exp(jax.random.uniform(derived_generator_seeds[1], (SAMPLE_TOTAL, ATTENTION_UNITS, 1), jnp.float32, math.log(0.1 / TOKEN_SPAN), math.log(1.0 / TOKEN_SPAN)))
    ambient_frequency = jnp.where(slow_mask, slow_rate, fast_rate)
    blocks = TOKEN_SPAN // TOK_DEV
    segment_amplitude = jnp.exp(jax.random.uniform(derived_generator_seeds[2], (SAMPLE_TOTAL, ATTENTION_UNITS, blocks, 1), jnp.float32, -0.7, 0.7))
    segment_amplitude = (segment_amplitude * jnp.ones((SAMPLE_TOTAL, ATTENTION_UNITS, blocks, TOK_DEV), jnp.float32)).reshape(SAMPLE_TOTAL, ATTENTION_UNITS, TOKEN_SPAN)
    stochastic_perturbation = jnp.exp(jax.random.uniform(derived_generator_seeds[3], (SAMPLE_TOTAL, ATTENTION_UNITS, TOKEN_SPAN), jnp.float32, -0.7, 0.7))
    spike_occurrences = jax.random.randint(derived_generator_seeds[4], (SAMPLE_TOTAL, ATTENTION_UNITS, TOKEN_SPAN), 0, max(TOKEN_SPAN // 4, 1)) == 0
    threshold_location = jax.random.uniform(derived_generator_seeds[5], (SAMPLE_TOTAL, ATTENTION_UNITS, TOKEN_SPAN), jnp.float32, 0.5, 0.8)
    return jnp.exp(-ambient_frequency * segment_amplitude * stochastic_perturbation) * jnp.where(spike_occurrences, threshold_location, 1.0)


def draw_beta(key, part):
    share = 500
    slow_mask = slow_heads(key, share)
    key = jax.random.fold_in(key, 23)
    derived_generator_seeds = jax.random.split(key, 3)
    slow_level = jnp.exp(jax.random.uniform(derived_generator_seeds[0], (SAMPLE_TOTAL, ATTENTION_UNITS, 1), jnp.float32, math.log(20.0 / TOKEN_SPAN), math.log(150.0 / TOKEN_SPAN)))
    fast_level = jax.random.uniform(derived_generator_seeds[1], (SAMPLE_TOTAL, ATTENTION_UNITS, 1), jnp.float32, 0.3, 0.9)
    level = jnp.where(slow_mask, slow_level, fast_level)
    stochastic_perturbation = jnp.exp(jax.random.uniform(derived_generator_seeds[2], (SAMPLE_TOTAL, ATTENTION_UNITS, TOKEN_SPAN), jnp.float32, -0.5, 0.5))
    return jnp.minimum(level * stochastic_perturbation, 1.0)


def strengthened(array, own_key, source, target, shards_of, factor):
    def block_of(axis_at):
        return (jnp.arange(array.shape[axis_at]) // (array.shape[axis_at] // shards_of)).reshape((-1,) + (1,) * (array.ndim - 1 - axis_at))

    one_side = jax.random.permutation(own_key, shards_of)[block_of(target)]
    second = (block_of(target) + shards_of // 2) % shards_of
    return jnp.where((block_of(source) == one_side) | (block_of(source) == second), factor * array, array)


def level_of(own_key, extent, cuts, smallest, top_value):
    factor_of, own = 1.0, jax.random.fold_in(own_key, 6)
    for position, parts in cuts:
        steps = jnp.exp(jax.random.uniform(jax.random.fold_in(own, position), (parts,), jnp.float32, smallest / len(cuts), top_value / len(cuts)))
        factor_of = factor_of * jnp.repeat(steps, extent[position] // parts).reshape([-1 if axis == position else 1 for axis in range(len(extent))])
    return factor_of


def scatter_about(key, extent, spread, bound, shards=(), kind=jnp.bfloat16):
    entries = jax.random.normal(key, extent, jnp.float32) * spread
    if len(shards) > 0:
        entries = level_of(key, extent, shards, -0.22, 0.18) * entries
    return jnp.clip(entries, min=-bound, max=bound).astype(kind)


def gaussian_with(own_key, extent, spread, reach, pieces, heavy, dtype=jnp.bfloat16):
    drawn = spread * jax.random.normal(own_key, extent, jnp.float32)
    if pieces:
        drawn = drawn * level_of(own_key, extent, pieces, -0.22, 0.18)
    return jnp.clip(strengthened(drawn, jax.random.fold_in(own_key, 3), *heavy), -reach, reach).astype(dtype)


def setup_inputs(seed: int = 0) -> dict:
    splits = jax.random.split(jax.random.key(seed), 8)
    return {
        "queries": scatter_about(splits[0], (SAMPLE_TOTAL, TOKEN_SPAN, ATTENTION_UNITS * DK), 1.0, 6.0, ((0, 4), (1, 2), (2, 4))),
        "keys": scatter_about(splits[1], (SAMPLE_TOTAL, TOKEN_SPAN, ATTENTION_UNITS * DK), 1.0, 6.0, ((0, 4), (1, 2), (2, 4))),
        "values": scatter_about(splits[2], (SAMPLE_TOTAL, TOKEN_SPAN, ATTENTION_UNITS * DK), 1.0, 6.0, ((0, 4), (1, 2), (2, 4))),
        "decay": draw_decay(jax.random.fold_in(splits[7], 71), 0),
        "beta": draw_beta(jax.random.fold_in(splits[7], 71), 0),
        "inputs": gaussian_with(splits[5], (SAMPLE_TOTAL, TOKEN_SPAN, D), 1.0, 6.0, ((0, 4), (1, 2)), (1, 2, 2, 2.0)),
        "probe": scatter_about(splits[6], (D, ATTENTION_UNITS * DK), D ** -0.5, 0.09375, ((0, 8), (1, 4))),
    }


EPSILON = 1e-06
EXACT = lax.Precision.HIGHEST

def normalize(block):
    return block * lax.rsqrt(lax.optimization_barrier(jnp.sum(block * block, -1, keepdims=True)) + EPSILON)

def reference(queries, keys, values, decay, beta, inputs, probe):
    batch_count, length, width = queries.shape
    head_count = width // DK

    def per_head(block):
        return jnp.moveaxis(block.astype(jnp.float32).reshape(batch_count, length, head_count, DK), 1, 0)
    flat_inputs = inputs.reshape(batch_count * length, D)
    tangent_full = jnp.dot(flat_inputs, probe, preferred_element_type=jnp.float32).reshape(batch_count, length, width)
    rounded = lax.optimization_barrier((normalize(per_head(queries)).astype(jnp.bfloat16), normalize(per_head(keys)).astype(jnp.bfloat16), tangent_full.astype(jnp.bfloat16)))
    queries_unit = rounded[0].astype(jnp.float32)
    keys_unit = rounded[1].astype(jnp.float32)
    tangent = rounded[2]
    paired = jnp.concatenate([per_head(values), per_head(tangent)], -1)
    decay_steps = jnp.moveaxis(decay, 2, 0)
    beta_steps = jnp.moveaxis(beta, 2, 0)

    def forward(memory, element):
        query_row, key_row, value_row, factor, strength = element
        recalled = jnp.einsum('bhvj,bhj->bhv', memory, key_row, precision=EXACT)
        kept = factor[..., None, None] * (memory - strength[..., None, None] * recalled[..., None] * key_row[:, :, None, :])
        memory = kept + strength[..., None, None] * value_row[..., None] * key_row[:, :, None, :]
        return (memory, jnp.einsum('bhvj,bhj->bhv', memory, query_row, precision=EXACT))
    start_state = jnp.zeros((batch_count, head_count, 2 * DK, DK), jnp.float32)
    unused, outputs = lax.scan(forward, start_state, (queries_unit, keys_unit, paired, decay_steps, beta_steps))
    mixed = jnp.moveaxis(outputs[..., :DK], 0, 1).reshape(batch_count, length, width).astype(jnp.bfloat16)
    weighting = math.sqrt(D) / (batch_count * length)
    grad_out = weighting * outputs[..., DK:]

    def backward(carried, element):
        query_row, key_row, grad_row, factor, strength = element
        adjoint = carried + grad_row[..., None] * query_row[:, :, None, :]
        recalled = jnp.einsum('bhvj,bhj->bhv', adjoint, key_row, precision=EXACT)
        grad_row_values = strength[..., None] * recalled
        carried = factor[..., None, None] * (adjoint - strength[..., None, None] * recalled[..., None] * key_row[:, :, None, :])
        return (carried, grad_row_values)
    start_grad = jnp.zeros((batch_count, head_count, DK, DK), jnp.float32)
    unused_grad, grad_values = lax.scan(backward, start_grad, (queries_unit, keys_unit, grad_out, decay_steps, beta_steps), reverse=True)
    grad_flat = jnp.moveaxis(grad_values, 0, 1).reshape(batch_count * length, width).astype(jnp.bfloat16)
    curvature = lax.dot_general(flat_inputs, grad_flat, (((0,), (0,)), ((), ())), preferred_element_type=jnp.float32)
    return (mixed, curvature)
```

```python
import functools
import math

import jax
import jax.numpy as jnp
from jax import lax
from jax.experimental import pallas as pl
from jax.experimental.pallas import tpu as pltpu
from jax.sharding import PartitionSpec as P

D = 4096
DK = 128
SPAN = 128
EPSILON = 1e-06
GROUP = ("dp", "ctx")
BF16 = jnp.bfloat16
F32 = jnp.float32
VMEM_BYTES = 48 * 1024 * 1024


def dot(left, right):
    return jnp.dot(left, right, preferred_element_type=F32)


def dot_nt(left, right):
    return lax.dot_general(left, right, (((1,), (1,)), ((), ())), preferred_element_type=F32)


def dot_tn(left, right):
    return lax.dot_general(left, right, (((0,), (0,)), ((), ())), preferred_element_type=F32)


def halves(block):
    high = block.astype(BF16)
    return high, (block - high.astype(F32)).astype(BF16)


def fine_dot(left, right):
    left_high, left_low = halves(left)
    right_high, right_low = halves(right)
    wide = jnp.concatenate([right_high, right_low], 1)
    both = dot(jnp.concatenate([left_high, left_low], 1), jnp.concatenate([wide, wide], 0))
    width = right.shape[1]
    return both[:, :width] + both[:, width:]


def unit(block):
    block = block.astype(F32)
    return (block * lax.rsqrt(jnp.sum(block * block, -1, keepdims=True) + EPSILON)).astype(BF16)


def prepare_kernel(with_state, heads, chunks, *refs):
    if with_state:
        place, *refs = refs
        (qm, km, vm, qt, kt, vt, decay_m, beta_m, decay_t, beta_t, first, mixed, forth, back, last, state) = refs
    else:
        place, *refs = refs
        (qm, km, vm, qt, kt, vt, decay_m, beta_m, decay_t, beta_t, mixed, forth, back, last, state) = refs
    step = pl.program_id(0)
    core = place[0]
    is_mine = (step // (pl.num_programs(0) // 2)) == core

    @pl.when(step == 0)
    def _():
        if with_state:
            state[...] = first[...]
        else:
            state[...] = jnp.zeros_like(state)

    rows = lax.broadcasted_iota(jnp.int32, (SPAN, SPAN), 0)
    cols = lax.broadcasted_iota(jnp.int32, (SPAN, SPAN), 1)
    inclusive = rows >= cols
    strict = rows > cols
    diagonal = rows == cols

    def pick(mine, theirs):
        return jnp.where(is_mine, mine, theirs)

    def gates(mine, theirs):
        block = pick(mine[0], theirs[0])
        return jnp.where(core == 0, block[:heads], block[heads:])

    decay_log = jnp.log(gates(decay_m, decay_t))
    strengths = gates(beta_m, beta_t)
    queries, keys, values = (
        pick(mine[0], theirs[0]) for mine, theirs in ((qm, qt), (km, kt), (vm, vt))
    )
    items = [(chunk, head) for chunk in range(chunks) for head in range(heads)]

    def cut(block, item):
        chunk, head = item
        return block[chunk * SPAN : (chunk + 1) * SPAN, head * DK : (head + 1) * DK]

    def cut_row(block, item):
        chunk, head = item
        return block[head : head + 1, chunk * SPAN : (chunk + 1) * SPAN]

    def column_of(row):
        return jnp.sum(jnp.where(diagonal, row, 0.0), 1, keepdims=True)

    def row_of(column):
        return jnp.sum(jnp.where(diagonal, column, 0.0), 0, keepdims=True)

    q = [unit(cut(queries, item)) for item in items]
    k = [unit(cut(keys, item)) for item in items]
    v = [cut(values, item) for item in items]
    growth_log = [
        jnp.sum(jnp.where(inclusive, cut_row(decay_log, item), 0.0), 1, keepdims=True) for item in items
    ]
    strength_row = [cut_row(strengths, item) for item in items]
    inner = [dot_nt(jnp.concatenate([kk, qq], 0), kk) for kk, qq in zip(k, q)]
    ratios = [
        jnp.where(inclusive, jnp.exp(jnp.where(inclusive, log - row_of(log), 0.0)), 0.0)
        for log in growth_log
    ]
    coupling = [
        jnp.where(strict, column_of(row) * ratio * both[:SPAN], 0.0)
        for row, ratio, both in zip(strength_row, ratios, inner)
    ]
    mixing = [ratio * both[SPAN:] for ratio, both in zip(ratios, inner)]

    def lower_left(size):
        return (rows // (2 * size) == cols // (2 * size)) & (
            (rows // size) % 2 == 1
        ) & ((cols // size) % 2 == 0)

    identity = jnp.where(diagonal, 1.0, 0.0)
    corner = lower_left(1)
    inverse = [identity - jnp.where(corner, block, 0.0) for block in coupling]
    size = 2
    while size < SPAN:
        corner = lower_left(size)
        narrow = [block.astype(BF16) for block in inverse]
        part = [dot(x, jnp.where(corner, a, 0.0).astype(BF16)) for x, a in zip(narrow, coupling)]
        step_back = [dot(y.astype(BF16), x) for y, x in zip(part, narrow)]
        inverse = [x - z for x, z in zip(inverse, step_back)]
        size *= 2
    residual = [identity - x - fine_dot(a, x) for a, x in zip(coupling, inverse)]
    inverse = [
        x + dot(x.astype(BF16), e.astype(BF16)) for x, e in zip(inverse, residual)
    ]
    scaled = [x * row for x, row in zip(inverse, strength_row)]
    growth = [jnp.exp(log) for log in growth_log]
    grown_keys = [g * kk.astype(F32) for g, kk in zip(growth, k)]
    grown_queries = [g * qq.astype(F32) for g, qq in zip(growth, q)]
    tails = [
        (jnp.exp(log[SPAN - 1 :] - log) * kk.astype(F32)).T for log, kk in zip(growth_log, k)
    ]
    upper = [
        fine_dot(jnp.concatenate([tail, mix], 0), b) for tail, mix, b in zip(tails, mixing, scaled)
    ]
    removed = [fine_dot(up, gk) for up, gk in zip(upper, grown_keys)]
    maps = []
    for g, up, rem, gq in zip(growth, upper, removed, grown_queries):
        kept = jnp.where(diagonal, g[SPAN - 1 :], 0.0)
        maps.append(jnp.concatenate([jnp.concatenate([kept, gq], 0) - rem, up], 1))
    for item, whole in zip(items, maps):
        chunk, head = item
        forth[chunk, head] = whole.astype(BF16)
        back[chunk, head] = whole.T.astype(BF16)
    for chunk in range(chunks):
        for head in range(heads):
            index = chunk * heads + head
            high, low = halves(maps[index])
            x_high, x_low = halves(state[head])
            zero = jnp.zeros_like(v[index])
            wide = jnp.concatenate(
                [jnp.concatenate([x_high, x_low], 1), jnp.concatenate([v[index], zero], 1)], 0
            )
            both = dot(high, wide)
            result = both[:, :DK] + both[:, DK:] + dot(low, wide[:, :DK])
            state[head] = result[:DK]
            mixed[chunk * SPAN : (chunk + 1) * SPAN, head * DK : (head + 1) * DK] = result[DK:].astype(BF16)

    @pl.when(step == pl.num_programs(0) - 1)
    def _():
        last[...] = state[...]


def prepare(core, own, other, first):
    tokens = own[0].shape[1]
    width = own[0].shape[2] // 2
    heads = width // DK
    chunks = 2
    length = chunks * SPAN
    per_device = tokens // length
    steps = 2 * per_device
    total = 2 * tokens // SPAN
    wide = pl.BlockSpec((1, length, width), lambda i, place: (0, i % per_device, place[0]))
    gate = pl.BlockSpec((1, 2 * heads, length), lambda i, place: (0, 0, i % per_device))
    states = pl.BlockSpec((heads, DK, DK), lambda i, place: (0, 0, 0))
    maps = pl.BlockSpec((chunks, heads, 2 * DK, 2 * DK), lambda i, place: (i, 0, 0, 0))
    extra = () if first is None else (first,)
    return pl.pallas_call(
        functools.partial(prepare_kernel, first is not None, heads, chunks),
        grid_spec=pltpu.PrefetchScalarGridSpec(
            num_scalar_prefetch=1,
            grid=(steps,),
            in_specs=[wide] * 6 + [gate] * 4 + [states] * len(extra),
            out_specs=[pl.BlockSpec((length, width), lambda i, place: (i, 0)), maps, maps, states],
            scratch_shapes=[pltpu.VMEM((heads, DK, DK), F32)],
        ),
        out_shape=[
            jax.ShapeDtypeStruct((2 * tokens, width), BF16),
            jax.ShapeDtypeStruct((total, heads, 2 * DK, 2 * DK), BF16),
            jax.ShapeDtypeStruct((total, heads, 2 * DK, 2 * DK), BF16),
            jax.ShapeDtypeStruct((heads, DK, DK), F32),
        ],
        compiler_params=pltpu.CompilerParams(vmem_limit_bytes=VMEM_BYTES),
        name="prepare",
    )(core, *own[:3], *other[:3], own[3], own[4], other[3], other[4], *extra)


def column_copies(place, first, count, rows, mine, theirs, buffer, sems):
    copies = []
    for index in range(count):
        start = pl.multiple_of(place[first + index] * rows, rows)
        for which, source in enumerate((mine, theirs)):
            copies.append(
                pltpu.make_async_copy(
                    source.at[:, pl.ds(start, rows)], buffer.at[index, which], sems.at[index, which]
                )
            )
    return copies


def tangent_kernel(count, place, mine, theirs, *refs):
    pieces, (total, buffer, sems) = refs[:count], refs[count:]
    tokens = mine.shape[0]
    rows = pieces[0].shape[0]
    copies = column_copies(place, 1, count, rows, mine, theirs, buffer, sems)
    for copy in copies:
        copy.start()
    core = place[0]
    offsets = [pl.multiple_of(core * tokens, tokens), pl.multiple_of((1 - core) * tokens, tokens)]
    for index in range(count):
        for which in range(2):
            copies[2 * index + which].wait()
            part = dot(buffer[index, which], pieces[index][...])
            place_rows = pl.ds(offsets[which], tokens)
            if index == 0:
                total[place_rows, :] = part
            else:
                total[place_rows, :] += part


def tangent(core, mine, theirs, blocks, pieces):
    count = len(pieces)
    rows, width = pieces[0].shape
    tokens = mine.shape[0]
    any_spec = pl.BlockSpec(memory_space=pl.ANY)
    vmem_spec = pl.BlockSpec(memory_space=pltpu.VMEM)
    return pl.pallas_call(
        functools.partial(tangent_kernel, count),
        grid_spec=pltpu.PrefetchScalarGridSpec(
            num_scalar_prefetch=1,
            grid=(),
            in_specs=[any_spec] * 2 + [vmem_spec] * count,
            out_specs=vmem_spec,
            scratch_shapes=[
                pltpu.VMEM((count, 2, tokens, rows), BF16),
                pltpu.SemaphoreType.DMA((count, 2)),
            ],
        ),
        out_shape=jax.ShapeDtypeStruct((2 * tokens, width), F32),
        compiler_params=pltpu.CompilerParams(vmem_limit_bytes=VMEM_BYTES),
        name="tangent",
    )(jnp.stack([core] + list(blocks)), mine, theirs, *pieces)


def recur_kernel(weighting, with_state, count, place, mine, theirs, total, forth, back, *refs):
    pieces, refs = refs[:count], refs[count:]
    if with_state:
        (first, final, *refs) = refs
    (grads, last, start, buffer, forth_in, back_in, tangent_in, up, sems, map_sems) = refs
    tokens = mine.shape[0]
    rows = pieces[0].shape[0]
    spans, heads = forth.shape[:2]
    copies = column_copies(place, 1, count, rows, mine, theirs, buffer, sems)
    for copy in copies:
        copy.start()
    forth_copy = pltpu.make_async_copy(forth, forth_in, map_sems.at[0])
    back_copy = pltpu.make_async_copy(back, back_in, map_sems.at[1])
    forth_copy.start()
    back_copy.start()
    core = place[0]
    for which, owner in enumerate((core, 1 - core)):
        place_rows = pl.ds(pl.multiple_of(owner * tokens, tokens), tokens)
        part = total[place_rows, :]
        for index in range(count):
            copies[2 * index + which].wait()
            part += dot(buffer[index, which], pieces[index][...])
        tangent_in[place_rows, :] = part.astype(BF16)
    forth_copy.wait()
    back_copy.wait()
    zero = jnp.zeros((DK, DK), F32)
    states = [first[head] if with_state else zero for head in range(heads)]
    for span in range(spans):
        for head in range(heads):
            block = tangent_in[span * SPAN : (span + 1) * SPAN, head * DK : (head + 1) * DK]
            fresh = dot(forth_in[span, head, :, DK:], block)
            result = dot(forth_in[span, head, :, :DK], states[head].astype(BF16)) + fresh
            states[head] = result[:DK]
            grad = (weighting * result[DK:]).astype(BF16)
            up[span, head] = dot(back_in[span, head, :, DK:], grad)
    for head in range(heads):
        last[head] = states[head]
    states = [final[head] if with_state else zero for head in range(heads)]
    for span in reversed(range(spans)):
        for head in range(heads):
            result = dot(back_in[span, head, :, :DK], states[head].astype(BF16)) + up[span, head]
            states[head] = result[:DK]
            grads[span * SPAN : (span + 1) * SPAN, head * DK : (head + 1) * DK] = result[DK:].astype(BF16)
    for head in range(heads):
        start[head] = states[head]


def recur(weighting, core, mine, theirs, total, forth, back, blocks, pieces, states):
    count = len(pieces)
    rows, width = pieces[0].shape
    tokens = mine.shape[0]
    spans, heads = forth.shape[:2]
    any_spec = pl.BlockSpec(memory_space=pl.ANY)
    vmem_spec = pl.BlockSpec(memory_space=pltpu.VMEM)
    extra = () if states is None else states
    return pl.pallas_call(
        functools.partial(recur_kernel, weighting, states is not None, count),
        grid_spec=pltpu.PrefetchScalarGridSpec(
            num_scalar_prefetch=1,
            grid=(),
            in_specs=[any_spec] * 2
            + [vmem_spec]
            + [any_spec] * 2
            + [vmem_spec] * (count + len(extra)),
            out_specs=[vmem_spec] * 3,
            scratch_shapes=[
                pltpu.VMEM((count, 2, tokens, rows), BF16),
                pltpu.VMEM(forth.shape, BF16),
                pltpu.VMEM(back.shape, BF16),
                pltpu.VMEM((2 * tokens, width), BF16),
                pltpu.VMEM((spans, heads, 2 * DK, DK), F32),
                pltpu.SemaphoreType.DMA((count, 2)),
                pltpu.SemaphoreType.DMA((2,)),
            ],
        ),
        out_shape=[
            jax.ShapeDtypeStruct((2 * tokens, width), BF16),
            jax.ShapeDtypeStruct((heads, DK, DK), F32),
            jax.ShapeDtypeStruct((heads, DK, DK), F32),
        ],
        compiler_params=pltpu.CompilerParams(vmem_limit_bytes=VMEM_BYTES),
        name="recur",
    )(jnp.stack([core] + list(blocks)), mine, theirs, total, forth, back, *pieces, *extra)


ROWS = 256


def curvature_kernel(counts, place, mine, theirs, grads, *refs):
    outs, (buffer, sems) = refs[: len(counts)], refs[len(counts) :]
    count = sum(counts)
    tokens = mine.shape[0]
    copies = column_copies(place, 1, count, ROWS, mine, theirs, buffer, sems)
    for copy in copies:
        copy.start()
    core = place[0]
    both = [
        grads[pl.ds(pl.multiple_of(owner * tokens, tokens), tokens), :] for owner in (core, 1 - core)
    ]
    index = 0
    for out, length in zip(outs, counts):
        for slot in range(length):
            copies[2 * index].wait()
            copies[2 * index + 1].wait()
            part = dot_tn(buffer[index, 0], both[0]) + dot_tn(buffer[index, 1], both[1])
            out[slot] = part.astype(out.dtype)
            index += 1


def curvature(core, mine, theirs, grads, blocks, types):
    counts = tuple(len(part) for part in blocks)
    tokens = mine.shape[0]
    width = grads.shape[1]
    any_spec = pl.BlockSpec(memory_space=pl.ANY)
    vmem_spec = pl.BlockSpec(memory_space=pltpu.VMEM)
    return pl.pallas_call(
        functools.partial(curvature_kernel, counts),
        grid_spec=pltpu.PrefetchScalarGridSpec(
            num_scalar_prefetch=1,
            grid=(),
            in_specs=[any_spec] * 2 + [vmem_spec],
            out_specs=[vmem_spec] * len(counts),
            scratch_shapes=[
                pltpu.VMEM((sum(counts), 2, tokens, ROWS), BF16),
                pltpu.SemaphoreType.DMA((sum(counts), 2)),
            ],
        ),
        out_shape=[
            jax.ShapeDtypeStruct((count, ROWS, width), kind) for count, kind in zip(counts, types)
        ],
        compiler_params=pltpu.CompilerParams(vmem_limit_bytes=VMEM_BYTES),
        name="curvature",
    )(jnp.stack([core] + [index for part in blocks for index in part]), mine, theirs, grads)


def local(square, dp_size, ctx_size, queries, keys, values, decay, beta, inputs, probe):
    tokens = queries.shape[1]
    width = queries.shape[2] // 2
    weighting = math.sqrt(D) / (dp_size * ctx_size * tokens)
    ctx = lax.axis_index("ctx")
    chip = lax.axis_index("dp")
    core = lax.rem(ctx, 2)
    groups = ctx_size // 2
    partner = [(index, index ^ 1) for index in range(ctx_size)]
    mine = inputs[0]

    def swap(block):
        return lax.ppermute(block, "ctx", partner)

    def send(block, chips, cores):
        pairs = [
            (2 * index + which, 2 * (index ^ chips) + (which ^ cores))
            for index in range(dp_size)
            for which in range(2)
        ]
        return lax.ppermute(block, GROUP, pairs)

    def part(block, index):
        return lax.dynamic_slice_in_dim(block, index * width, width, 1)

    own = (queries, keys, values, decay, beta)
    if square:
        kept = part(probe, core)
        given = part(probe, 1 - core)
        x_one = send(kept, 1, 0)
        y_one = send(given, 2, 1)
        other = tuple(swap(block) for block in own)
        inside = swap(given)
        x_two = send(given, 1, 1)
        y_two = send(kept, 2, 0)
        theirs = swap(mine)
        far_one = send(x_one, 2, 0)
        far_two = send(y_one, 1, 0)
        pieces = [kept, inside, x_one, y_one, x_two, y_two, far_one, far_two]

        def block_at(chips, cores):
            return 2 * (chip ^ chips) + (core ^ cores)

        places = [
            block_at(0, 0),
            block_at(0, 1),
            block_at(1, 0),
            block_at(2, 1),
            block_at(1, 1),
            block_at(2, 0),
            block_at(3, 0),
            block_at(3, 1),
        ]
    else:
        other = tuple(swap(block) for block in own)
        theirs = swap(mine)
        gathered = part(lax.all_gather(probe, GROUP, axis=0, tiled=True), core)
        places = list(range(8))
        rows = D // len(places)
        pieces = [gathered[index * rows : (index + 1) * rows] for index in places]
    places = [jnp.asarray(index, jnp.int32) for index in places]

    def shift(block, by):
        pairs = [
            (index, index + 2 * by)
            for index in range(ctx_size)
            if 0 <= index + 2 * by < ctx_size
        ]
        return lax.ppermute(block, "ctx", pairs)

    early = len(pieces) - 2
    entry = None
    if groups > 1:
        entry = jnp.zeros((width // DK, DK, DK), F32)
        for _ in range(groups - 1):
            entry = shift(prepare(core[None], own, other, entry)[3], 1)
    read, forth, back, unused = prepare(core[None], own, other, entry)
    read_swapped = swap(lax.dynamic_slice_in_dim(read, (1 - core) * tokens, tokens, 0))
    read_kept = lax.dynamic_slice_in_dim(read, core * tokens, tokens, 0)
    mixed = jnp.where(
        core == 0,
        jnp.concatenate([read_kept, read_swapped], 1),
        jnp.concatenate([read_swapped, read_kept], 1),
    )
    total = tangent(core, mine, theirs, places[:early], pieces[:early])
    run = functools.partial(
        recur, weighting, core, mine, theirs, total, forth, back, places[early:], pieces[early:]
    )
    states = None
    if groups > 1:
        states = (jnp.zeros((width // DK, DK, DK), F32),) * 2
        for _ in range(groups - 1):
            states = (shift(run(states)[1], 1), states[1])
        for _ in range(groups - 1):
            states = (states[0], shift(run(states)[2], -1))
    grads = run(states)[0]
    build = functools.partial(curvature, core, mine, theirs, grads)
    if not square:
        everything = build([[jnp.int32(index) for index in range(D // ROWS)]], [F32])[0]
        flat = everything.reshape(D, width)
        zero = jnp.zeros_like(flat)
        both = jnp.where(
            core == 0, jnp.concatenate([flat, zero], 1), jnp.concatenate([zero, flat], 1)
        )
        return mixed[None], lax.psum_scatter(both, GROUP, scatter_dimension=0, tiled=True)

    def rows_at(chips, half):
        return [4 * (chip ^ chips) + 2 * which + half for which in range(2)]

    far_x, far_y = build([rows_at(3, 0), rows_at(3, 1)], [BF16] * 2)
    far_x = send(far_x, 1, 0)
    far_y = send(far_y, 2, 0)
    near_x, near_y = build([rows_at(1, 0), rows_at(2, 1)], [BF16] * 2)
    near_x = send(near_x, 1, 0)
    near_y = send(near_y, 2, 0)
    keep_y, keep_x, own_top, own_low = build(
        [rows_at(2, 0), rows_at(1, 1), rows_at(0, 0), rows_at(0, 1)], [F32] * 4
    )

    def at(block, index):
        return lax.dynamic_index_in_dim(block, index, 0, keepdims=False)

    relay_y = (keep_y + far_x.astype(F32)).astype(BF16)
    relay_x = (keep_x + far_y.astype(F32)).astype(BF16)
    top_same = send(at(relay_y, core), 2, 0)
    low_same = send(at(relay_x, core), 1, 0)
    top_cross = send(at(relay_y, 1 - core), 2, 1)
    low_cross = send(at(relay_x, 1 - core), 1, 1)
    sum_top = own_top + near_x.astype(F32)
    sum_low = own_low + near_y.astype(F32)
    sums = jnp.concatenate([sum_top, sum_low], 1)
    across = swap(at(sums, 1 - core))
    near = at(sums, core) + jnp.concatenate([top_same, low_same], 0).astype(F32)
    distant = across + jnp.concatenate([top_cross, low_cross], 0).astype(F32)
    result = jnp.where(
        core == 0, jnp.concatenate([near, distant], 1), jnp.concatenate([distant, near], 1)
    )
    return mixed[None], result


def solution(mesh):
    dp_size, ctx_size = mesh.shape["dp"], mesh.shape["ctx"]
    square = dp_size == 4 and ctx_size == 2
    return jax.shard_map(
        functools.partial(local, square, dp_size, ctx_size),
        mesh=mesh,
        in_specs=(
            P("dp", "ctx", "head"),
            P("dp", "ctx", "head"),
            P("dp", "ctx", "head"),
            P("dp", "head", "ctx"),
            P("dp", "head", "ctx"),
            P("dp", "ctx", None),
            P(("dp", "ctx"), "head"),
        ),
        out_specs=(P("dp", "ctx", "head"), P(("dp", "ctx"), "head")),
        check_vma=False,
    )
```

```python
import functools
import math

import jax
import jax.numpy as jnp
from jax import lax
from jax.experimental import pallas as pl
from jax.experimental.pallas import tpu as pltpu
from jax.sharding import PartitionSpec as P

D = 4096
DK = 128
SPAN = 128
EPSILON = 1e-06
GROUP = ("dp", "ctx")
BF16 = jnp.bfloat16
F32 = jnp.float32
VMEM_BYTES = 24 * 1024 * 1024


def cost(us):
    return pl.CostEstimate(flops=int(us * 1.1e9), bytes_accessed=int(us * 3.0e6), transcendentals=0)


def in_hbm(block):
    return pltpu.with_memory_space_constraint(block, pltpu.HBM)


def in_vmem(block):
    return pltpu.with_memory_space_constraint(block, pltpu.VMEM)


def kernel_call(kernel, name, place, operands, outs, scratch=(), aliases=None, far=()):
    vmem_spec = pl.BlockSpec(memory_space=pltpu.VMEM)
    return pl.pallas_call(
        kernel,
        grid_spec=pltpu.PrefetchScalarGridSpec(
            num_scalar_prefetch=1,
            grid=(),
            in_specs=[pl.BlockSpec(memory_space=pltpu.HBM)] * len(far) + [vmem_spec] * len(operands),
            out_specs=[vmem_spec] * len(outs),
            scratch_shapes=list(scratch),
        ),
        out_shape=[jax.ShapeDtypeStruct(shape, kind) for shape, kind in outs],
        input_output_aliases=aliases or {},
        compiler_params=pltpu.CompilerParams(vmem_limit_bytes=VMEM_BYTES),
        cost_estimate=cost(0.01),
        name=name,
    )(place, *(in_hbm(block) for block in far), *(in_vmem(block) for block in operands))


def dot(left, right):
    return jnp.dot(left, right, preferred_element_type=F32)


def dot_nt(left, right):
    return lax.dot_general(left, right, (((1,), (1,)), ((), ())), preferred_element_type=F32)


def dot_tn(left, right):
    return lax.dot_general(left, right, (((0,), (0,)), ((), ())), preferred_element_type=F32)


def halves(block):
    high = block.astype(BF16)
    return high, (block - high.astype(F32)).astype(BF16)


def fine_dot(left, right):
    left_high, left_low = halves(left)
    right_high, right_low = halves(right)
    wide = jnp.concatenate([right_high, right_low], 1)
    both = dot(jnp.concatenate([left_high, left_low], 1), jnp.concatenate([wide, wide], 0))
    width = right.shape[1]
    return both[:, :width] + both[:, width:]


def unit(block):
    block = block.astype(F32)
    return (block * lax.rsqrt(jnp.sum(block * block, -1, keepdims=True) + EPSILON)).astype(BF16)


def pack_kernel(place, queries, keys, values, decay, beta, probe, kept, given, own, stack, gates, sems):
    core = place[0]
    width = kept.shape[1]
    same = pl.ds(pl.multiple_of(core * width, width), width)
    cross = pl.ds(pl.multiple_of((1 - core) * width, width), width)
    moves = [(probe.at[:, same], kept), (probe.at[:, cross], given)]
    moves += [(block.at[0, :, cross], stack.at[i]) for i, block in enumerate((queries, keys, values))]
    moves += [(block.at[0, :, same], own.at[i]) for i, block in enumerate((queries, keys, values))]
    if stack.shape[0] > 3:
        moves.append((probe.at[:, cross], stack.at[3]))
    moves += [(decay.at[0], gates.at[0]), (beta.at[0], gates.at[1])]
    copies = [
        pltpu.make_async_copy(source, target, sems.at[i]) for i, (source, target) in enumerate(moves)
    ]
    for copy in copies:
        copy.start()
    for copy in copies:
        copy.wait()


def pack(place, with_probe, queries, keys, values, decay, beta, probe):
    tokens = queries.shape[1]
    width = queries.shape[2] // 2
    hbm_spec = pl.BlockSpec(memory_space=pltpu.HBM)
    vmem_spec = pl.BlockSpec(memory_space=pltpu.VMEM)
    half = jax.ShapeDtypeStruct((probe.shape[0], width), BF16)
    return pl.pallas_call(
        pack_kernel,
        grid_spec=pltpu.PrefetchScalarGridSpec(
            num_scalar_prefetch=1,
            grid=(),
            in_specs=[hbm_spec] * 6,
            out_specs=[vmem_spec] * 5,
            scratch_shapes=[pltpu.SemaphoreType.DMA((11,))],
        ),
        out_shape=[
            half,
            half,
            jax.ShapeDtypeStruct((3, tokens, width), BF16),
            jax.ShapeDtypeStruct((4 if with_probe else 3, tokens, width), BF16),
            jax.ShapeDtypeStruct((2,) + decay.shape[1:], F32),
        ],
        compiler_params=pltpu.CompilerParams(vmem_limit_bytes=VMEM_BYTES),
        cost_estimate=cost(0.01),
        name="pack",
    )(place, *(in_hbm(block) for block in (queries, keys, values, decay, beta, probe)))


def prepare_kernel(side, place, stack, gates, *refs):
    forth, forth_low, back = refs[-3:]
    core = place[0]
    owner = core if side == 0 else 1 - core
    queries, keys = stack[0], stack[1]
    tokens, width = queries.shape
    spans, heads = tokens // SPAN, width // DK
    rows = lax.broadcasted_iota(jnp.int32, (SPAN, SPAN), 0)
    cols = lax.broadcasted_iota(jnp.int32, (SPAN, SPAN), 1)
    inclusive = rows >= cols
    strict = rows > cols
    diagonal = rows == cols
    items = [(span, head) for span in range(spans) for head in range(heads)]

    def gate(index):
        return jnp.where(core == 0, gates[index, :heads], gates[index, heads:])

    def cut(block, item):
        span, head = item
        return block[span * SPAN : (span + 1) * SPAN, head * DK : (head + 1) * DK]

    def cut_row(block, item):
        span, head = item
        return block[head : head + 1, span * SPAN : (span + 1) * SPAN]

    def column_of(row):
        return jnp.sum(jnp.where(diagonal, row, 0.0), 1, keepdims=True)

    def row_of(column):
        return jnp.sum(jnp.where(diagonal, column, 0.0), 0, keepdims=True)

    def lower_left(size):
        return (
            (rows // (2 * size) == cols // (2 * size))
            & ((rows // size) % 2 == 1)
            & ((cols // size) % 2 == 0)
        )

    decay_log = jnp.log(gate(0))
    strengths = gate(1)
    identity = jnp.where(diagonal, 1.0, 0.0)

    def build(items):
        q = [unit(cut(queries, item)) for item in items]
        k = [unit(cut(keys, item)) for item in items]
        growth_log = [
            jnp.sum(jnp.where(inclusive, cut_row(decay_log, item), 0.0), 1, keepdims=True)
            for item in items
        ]
        strength_row = [cut_row(strengths, item) for item in items]
        inner = [dot_nt(jnp.concatenate([kk, qq], 0), kk) for kk, qq in zip(k, q)]
        ratios = [
            jnp.where(inclusive, jnp.exp(jnp.where(inclusive, log - row_of(log), 0.0)), 0.0)
            for log in growth_log
        ]
        coupling = [
            jnp.where(strict, column_of(row) * ratio * both[:SPAN], 0.0)
            for row, ratio, both in zip(strength_row, ratios, inner)
        ]
        mixing = [ratio * both[SPAN:] for ratio, both in zip(ratios, inner)]
        corner = lower_left(1)
        inverse = [identity - jnp.where(corner, block, 0.0) for block in coupling]
        size = 2
        while size < SPAN:
            corner = lower_left(size)
            narrow = [block.astype(BF16) for block in inverse]
            part = [
                dot(x, jnp.where(corner, a, 0.0).astype(BF16)) for x, a in zip(narrow, coupling)
            ]
            step_back = [dot(y.astype(BF16), x) for y, x in zip(part, narrow)]
            inverse = [x - z for x, z in zip(inverse, step_back)]
            size *= 2
        residual = [identity - x - fine_dot(a, x) for a, x in zip(coupling, inverse)]
        inverse = [x + dot(x.astype(BF16), e.astype(BF16)) for x, e in zip(inverse, residual)]
        scaled = [x * row for x, row in zip(inverse, strength_row)]
        growth = [jnp.exp(log) for log in growth_log]
        grown_keys = [g * kk.astype(F32) for g, kk in zip(growth, k)]
        grown_queries = [g * qq.astype(F32) for g, qq in zip(growth, q)]
        tails = [
            (jnp.exp(log[SPAN - 1 :] - log) * kk.astype(F32)).T for log, kk in zip(growth_log, k)
        ]
        upper = [
            fine_dot(jnp.concatenate([tail, mix], 0), b)
            for tail, mix, b in zip(tails, mixing, scaled)
        ]
        removed = [fine_dot(up, gk) for up, gk in zip(upper, grown_keys)]
        for item, g, up, rem, gq in zip(items, growth, upper, removed, grown_queries):
            span, head = item
            kept = jnp.where(diagonal, g[SPAN - 1 :], 0.0)
            whole = jnp.concatenate([jnp.concatenate([kept, gq], 0) - rem, up], 1)
            high, low = halves(whole)
            forth[owner, span, head] = high
            forth_low[owner, span, head] = low
            back[owner, span, head] = whole.T.astype(BF16)

    for start in range(0, len(items), BATCH):
        build(items[start : start + BATCH])


BATCH = 8


def prepare(place, side, stack, gates, maps):
    tokens = stack.shape[1]
    heads = gates.shape[1] // 2
    shape = (2, tokens // SPAN, heads, 2 * DK, 2 * DK)
    return kernel_call(
        functools.partial(prepare_kernel, side),
        "prepare",
        place,
        (stack, gates) + tuple(maps),
        [(shape, BF16)] * 3,
        aliases={3 + index: index for index in range(len(maps))},
    )


def owned(place, blocks):
    mine, theirs = blocks
    first = place[0] == 0
    return jnp.where(first, mine, theirs), jnp.where(first, theirs, mine)


def row_block(place, block):
    if isinstance(block, int):
        return block
    chips, core = block
    if core == "same":
        core = place[0]
    elif core == "other":
        core = 1 - place[0]
    return 2 * lax.bitwise_xor(place[1], chips) + core


def columns_of(place, block, width):
    return pl.ds(pl.multiple_of(row_block(place, block) * width, width), width)


def positions_of(owner, tokens):
    return pl.ds(pl.multiple_of(owner * tokens, tokens), tokens)


def load_piece(ref):
    return ref[...] if len(ref.shape) == 2 else ref[3]


def read_kernel(with_state, blocks, place, mine, theirs, own, stack, forth, low, *refs):
    count = len(blocks)
    pieces, refs = refs[:count], refs[count:]
    if with_state:
        (first, *refs) = refs
    (total, kept, given, last, read) = refs
    tokens, width = own.shape[1:]
    spans, heads = forth.shape[1:3]
    core = place[0]
    values = owned(place, (own[2], stack[2]))
    zero = jnp.zeros((DK, DK), F32)
    states = [first[head] if with_state else zero for head in range(heads)]
    for half in range(2):
        for span in range(spans):
            for head in range(heads):
                positions = slice(span * SPAN, (span + 1) * SPAN)
                columns = slice(head * DK, (head + 1) * DK)
                block = values[half][positions, columns]
                x_high, x_low = halves(states[head])
                wide = jnp.concatenate(
                    [
                        jnp.concatenate([x_high, x_low], 1),
                        jnp.concatenate([block, jnp.zeros_like(block)], 1),
                    ],
                    0,
                )
                both = dot(forth[half, span, head], wide)
                result = both[:, :DK] + both[:, DK:] + dot(low[half, span, head], wide[:, :DK])
                states[head] = result[:DK]
                read[half, positions, columns] = result[DK:].astype(BF16)
    for head in range(heads):
        last[head] = states[head]
    kept[...] = read[core]
    given[...] = read[1 - core]
    add_products(place, blocks, mine, theirs, pieces, total, None)


def paired(blocks):
    return not isinstance(blocks[0], int) and blocks[0][0] == blocks[1][0]


def add_products(place, blocks, mine, theirs, pieces, result, total):
    tokens = mine.shape[0]
    rows = mine.shape[1] // 8
    core = place[0]
    probe = [load_piece(piece) for piece in pieces]
    for source, owner in ((mine, core), (theirs, 1 - core)):
        positions = positions_of(owner, tokens)
        begin = 0
        part = None if total is None else total[positions, :]
        if paired(blocks):
            chip = lax.bitwise_xor(place[1], blocks[0][0])
            columns = pl.ds(pl.multiple_of(chip * 2 * rows, 2 * rows), 2 * rows)
            product = dot(source[:, columns], jnp.concatenate(owned(place, probe[:2]), 0))
            part = product if part is None else part + product
            begin = 2
        for block, piece in zip(blocks[begin:], probe[begin:]):
            product = dot(source[:, columns_of(place, block, rows)], piece)
            part = product if part is None else part + product
        result[positions, :] = part.astype(result.dtype)


def read_values(place, mine, theirs, own, stack, maps, blocks, pieces, entry):
    tokens, width = own.shape[1:]
    heads = width // DK
    extra = () if entry is None else (entry,)
    return kernel_call(
        functools.partial(read_kernel, entry is not None, tuple(blocks)),
        "read_values",
        place,
        (mine, theirs, own, stack, maps[0], maps[1], *pieces, *extra),
        [
            ((2 * tokens, width), F32),
            ((tokens, width), BF16),
            ((tokens, width), BF16),
            ((heads, DK, DK), F32),
        ],
        scratch=[pltpu.VMEM((2, tokens, width), BF16)],
    )


def recur_kernel(weighting, with_state, blocks, chips, lists, place, mine, theirs, total, forth, back, *refs):
    count = len(blocks)
    pieces, refs = refs[:count], refs[count:]
    if with_state:
        (first, final, *refs) = refs
    (grads, last, start, *refs) = refs
    shares, (sums, up) = refs[: len(lists)], refs[len(lists) :]
    tokens = mine.shape[0]
    spans, heads = forth.shape[1:3]
    add_products(place, blocks, mine, theirs, pieces, sums, total)
    zero = jnp.zeros((DK, DK), F32)
    states = [first[head] if with_state else zero for head in range(heads)]
    steps = [(half, span) for half in range(2) for span in range(spans)]
    for half, span in steps:
        begin = half * tokens + span * SPAN
        for head in range(heads):
            block = sums[begin : begin + SPAN, head * DK : (head + 1) * DK]
            fresh = dot(forth[half, span, head, :, DK:], block)
            result = dot(forth[half, span, head, :, :DK], states[head].astype(BF16)) + fresh
            states[head] = result[:DK]
            grad = (weighting * result[DK:]).astype(BF16)
            up[half, span, head] = dot(back[half, span, head, :, DK:], grad)
    for head in range(heads):
        last[head] = states[head]
    states = [final[head] if with_state else zero for head in range(heads)]
    for half, span in reversed(steps):
        begin = half * tokens + span * SPAN
        for head in range(heads):
            result = dot(back[half, span, head, :, :DK], states[head].astype(BF16))
            result = result + up[half, span, head]
            states[head] = result[:DK]
            grads[begin : begin + SPAN, head * DK : (head + 1) * DK] = result[DK:].astype(BF16)
    for head in range(heads):
        start[head] = states[head]
    if lists:
        put_products(place, chips, lists, mine, theirs, grads, shares)


def put_products(place, chips, lists, mine, theirs, grads, outs):
    tokens, width = mine.shape
    if chips is None:
        columns = pl.ds(0, width)
    else:
        columns = pl.ds(pl.multiple_of(lax.bitwise_xor(place[1], chips) * 4 * ROWS, 4 * ROWS), 4 * ROWS)
    core = place[0]
    part = dot_tn(mine[:, columns], grads[positions_of(core, tokens), :])
    part += dot_tn(theirs[:, columns], grads[positions_of(1 - core, tokens), :])
    for out, indices in zip(outs, lists):
        for slot, index in enumerate(indices):
            out[slot] = part[index * ROWS : (index + 1) * ROWS].astype(out.dtype)


def recur(weighting, place, mine, theirs, total, maps, blocks, pieces, chips, lists, states):
    tokens = mine.shape[0]
    width = total.shape[1]
    spans, heads = maps[0].shape[1:3]
    extra = () if states is None else states
    return kernel_call(
        functools.partial(
            recur_kernel, weighting, states is not None, tuple(blocks), chips, lists
        ),
        "recur",
        place,
        (mine, theirs, total, maps[0], maps[2], *pieces, *extra),
        [((2 * tokens, width), BF16), ((heads, DK, DK), F32), ((heads, DK, DK), F32)]
        + [((len(part), ROWS, width), BF16) for part in lists],
        scratch=[
            pltpu.VMEM((2 * tokens, width), BF16),
            pltpu.VMEM((2, spans, heads, 2 * DK, DK), F32),
        ],
    )


ROWS = 256


def curvature_kernel(jobs, place, mine, theirs, grads, *outs):
    begin = 0
    for chips, lists in jobs:
        put_products(place, chips, lists, mine, theirs, grads, outs[begin : begin + len(lists)])
        begin += len(lists)


def curvature(place, mine, theirs, grads, jobs, types):
    width = grads.shape[1]
    lengths = [len(part) for chips, lists in jobs for part in lists]
    return kernel_call(
        functools.partial(curvature_kernel, jobs),
        "curvature",
        place,
        (mine, theirs, grads),
        [((length, ROWS, width), kind) for length, kind in zip(lengths, types)],
    )


def join_kernel(place, *refs):
    core = place[0]
    count = len(refs) // 3
    for index in range(count):
        same, cross, whole = refs[2 * index], refs[2 * index + 1], refs[2 * count + index]
        width = same.shape[1]
        whole[:, positions_of(core, width)] = same[...]
        whole[:, positions_of(1 - core, width)] = cross[...]


def join(place, *pairs):
    return kernel_call(
        join_kernel,
        "join",
        place,
        [block for pair in pairs for block in pair],
        [((same.shape[0], 2 * same.shape[1]), same.dtype) for same, cross in pairs],
    )


def local(square, dp_size, ctx_size, queries, keys, values, decay, beta, inputs, probe):
    tokens = queries.shape[1]
    width = queries.shape[2] // 2
    weighting = math.sqrt(D) / (dp_size * ctx_size * tokens)
    ctx = lax.axis_index("ctx")
    chip = lax.axis_index("dp")
    core = lax.rem(ctx, 2)
    groups = ctx_size // 2
    partner = [(index, index ^ 1) for index in range(ctx_size)]
    mine = inputs[0]
    place = jnp.stack([core, chip])

    def swap(block):
        return lax.ppermute(block, "ctx", partner)

    def send(block, chips, cores):
        pairs = [
            (2 * index + which, 2 * (index ^ chips) + (which ^ cores))
            for index in range(dp_size)
            for which in range(2)
        ]
        return lax.ppermute(block, GROUP, pairs)

    def part(block, index):
        return lax.dynamic_slice_in_dim(block, index * width, width, 1)

    kept, given, own, stack, gates = pack(place, square, queries, keys, values, decay, beta, probe)
    gates, mine = lax.optimization_barrier((gates, mine))
    gates_t = swap(gates)
    if square:
        x_one = send(kept, 1, 0)
        y_one = send(given, 2, 1)
        stack = swap(stack)
        theirs = swap(mine)
        stack, kept, given = lax.optimization_barrier((stack, kept, given))
        x_two = send(given, 1, 1)
        y_two = send(kept, 2, 0)
        maps = prepare(place, 0, own, gates, ())
        x_one, y_one, *maps = lax.optimization_barrier((x_one, y_one, *maps))
        far_one = send(x_one, 2, 0)
        far_two = send(y_one, 1, 0)
        maps = prepare(place, 1, stack, gates_t, maps)
        pieces = [kept, stack, x_one, y_one, far_one, far_two, x_two, y_two]
        places = [
            (0, "same"),
            (0, "other"),
            (1, "same"),
            (2, "other"),
            (3, "same"),
            (3, "other"),
            (1, "other"),
            (2, "same"),
        ]
    else:
        stack = swap(stack)
        theirs = swap(mine)
        maps = prepare(place, 0, own, gates, ())
        maps = prepare(place, 1, stack, gates_t, maps)
        gathered = part(lax.all_gather(probe, GROUP, axis=0, tiled=True), core)
        places = list(range(8))
        rows = D // len(places)
        pieces = [gathered[index * rows : (index + 1) * rows] for index in places]
    def shift(block, by):
        pairs = [
            (index, index + 2 * by)
            for index in range(ctx_size)
            if 0 <= index + 2 * by < ctx_size
        ]
        return lax.ppermute(block, "ctx", pairs)

    entry = None
    if groups > 1:
        entry = jnp.zeros((width // DK, DK, DK), F32)
    read = functools.partial(
        read_values,
        place,
        mine,
        theirs,
        own,
        stack,
        maps,
        places[:4],
        pieces[:4],
    )
    for _ in range(groups - 1):
        entry = shift(read(entry)[3], 1)
    total, read_kept, read_given, unused = read(entry)
    read_swapped = swap(read_given)
    lists = ((0, 2), (1, 3)) if square else ()
    run = functools.partial(
        recur,
        weighting,
        place,
        mine,
        theirs,
        total,
        maps,
        places[4:],
        pieces[4:],
        3,
        lists,
    )
    states = None
    if groups > 1:
        states = (jnp.zeros((width // DK, DK, DK), F32),) * 2
        for _ in range(groups - 1):
            states = (shift(run(states)[1], 1), states[1])
        for _ in range(groups - 1):
            states = (states[0], shift(run(states)[2], -1))
    grads, unused, unused, *shares = run(states)
    build = functools.partial(curvature, place, mine, theirs, grads)
    if not square:
        everything = build(((None, (tuple(range(D // ROWS)),)),), [F32])[0]
        flat = everything.reshape(D, width)
        zero = jnp.zeros_like(flat)
        both = jnp.where(
            core == 0, jnp.concatenate([flat, zero], 1), jnp.concatenate([zero, flat], 1)
        )
        mixed = join(place, (read_kept, read_swapped))[0]
        return mixed[None], lax.psum_scatter(both, GROUP, scatter_dimension=0, tiled=True)

    far_x = send(shares[0], 1, 0)
    far_y = send(shares[1], 2, 0)
    upper, lower = (0, 2), (1, 3)
    near_x, keep_x, keep_y, near_y, own_top, own_low = build(
        ((1, (upper, lower)), (2, (upper, lower)), (0, (upper, lower))),
        [BF16, F32, F32, BF16, F32, F32],
    )
    near_x = send(near_x, 1, 0)
    near_y = send(near_y, 2, 0)
    far_x, far_y = lax.optimization_barrier((far_x, far_y))
    relay_y = send((keep_y + far_x.astype(F32)).astype(BF16), 2, 0)
    relay_x = send((keep_x + far_y.astype(F32)).astype(BF16), 1, 0)
    near_x, near_y, relay_x, relay_y = lax.optimization_barrier((near_x, near_y, relay_x, relay_y))
    top = own_top + near_x.astype(F32) + relay_y.astype(F32)
    low = own_low + near_y.astype(F32) + relay_x.astype(F32)
    sums = jnp.concatenate([top, low], 1)

    def at(block, index):
        return lax.dynamic_index_in_dim(block, index, 0, keepdims=False)

    near = at(sums, core)
    distant = swap(at(sums, 1 - core))
    mixed, result = join(place, (read_kept, read_swapped), (near, distant))
    return mixed[None], result


def solution(mesh):
    dp_size, ctx_size = mesh.shape["dp"], mesh.shape["ctx"]
    square = dp_size == 4 and ctx_size == 2
    return jax.shard_map(
        functools.partial(local, square, dp_size, ctx_size),
        mesh=mesh,
        in_specs=(
            P("dp", "ctx", "head"),
            P("dp", "ctx", "head"),
            P("dp", "ctx", "head"),
            P("dp", "head", "ctx"),
            P("dp", "head", "ctx"),
            P("dp", "ctx", None),
            P(("dp", "ctx"), "head"),
        ),
        out_specs=(P("dp", "ctx", "head"), P(("dp", "ctx"), "head")),
        check_vma=False,
    )
```

```python
import functools
import math

import jax
import jax.numpy as jnp
from jax import lax
from jax.experimental import pallas as pl
from jax.experimental.pallas import tpu as pltpu
from jax.sharding import PartitionSpec as P

D = 4096
DK = 128
SPAN = 128
EPSILON = 1e-06
GROUP = ("dp", "ctx")
BF16 = jnp.bfloat16
F32 = jnp.float32
VMEM_BYTES = 24 * 1024 * 1024


def cost(us):
    return pl.CostEstimate(flops=int(us * 1.1e9), bytes_accessed=int(us * 3.0e6), transcendentals=0)


def in_hbm(block):
    return pltpu.with_memory_space_constraint(block, pltpu.HBM)


def in_vmem(block):
    return pltpu.with_memory_space_constraint(block, pltpu.VMEM)


def kernel_call(kernel, name, place, operands, outs, scratch=(), aliases=None, far=()):
    vmem_spec = pl.BlockSpec(memory_space=pltpu.VMEM)
    return pl.pallas_call(
        kernel,
        grid_spec=pltpu.PrefetchScalarGridSpec(
            num_scalar_prefetch=1,
            grid=(),
            in_specs=[pl.BlockSpec(memory_space=pltpu.HBM)] * len(far) + [vmem_spec] * len(operands),
            out_specs=[vmem_spec] * len(outs),
            scratch_shapes=list(scratch),
        ),
        out_shape=[jax.ShapeDtypeStruct(shape, kind) for shape, kind in outs],
        input_output_aliases=aliases or {},
        compiler_params=pltpu.CompilerParams(vmem_limit_bytes=VMEM_BYTES),
        cost_estimate=cost(0.01),
        name=name,
    )(place, *(in_hbm(block) for block in far), *(in_vmem(block) for block in operands))


def dot(left, right):
    return jnp.dot(left, right, preferred_element_type=F32)


def dot_nt(left, right):
    return lax.dot_general(left, right, (((1,), (1,)), ((), ())), preferred_element_type=F32)


def halves(block):
    high = block.astype(BF16)
    return high, (block - high.astype(F32)).astype(BF16)


def fine_dot(left, right):
    left_high, left_low = halves(left)
    right_high, right_low = halves(right)
    wide = jnp.concatenate([right_high, right_low], 1)
    both = dot(jnp.concatenate([left_high, left_low], 1), jnp.concatenate([wide, wide], 0))
    width = right.shape[1]
    return both[:, :width] + both[:, width:]


def unit(block):
    block = block.astype(F32)
    return (block * lax.rsqrt(jnp.sum(block * block, -1, keepdims=True) + EPSILON)).astype(BF16)


GATE_ROWS = 32


def terms_of(block):
    terms = []
    for _ in range(3):
        term = block.astype(BF16)
        terms.append(term.astype(F32))
        block = block - terms[-1]
    return terms


def pack_kernel(place, queries, keys, values, decay, beta, probe, kept, given, own, stack, gates, sems):
    core = place[0]
    tokens, width = own.shape[1:]
    same = pl.ds(pl.multiple_of(core * width, width), width)
    cross = pl.ds(pl.multiple_of((1 - core) * width, width), width)
    slots = [pl.ds(i * tokens, tokens) for i in range(4)]
    moves = [(decay.at[0], gates.at[0]), (beta.at[0], gates.at[1])]
    moves += [(probe.at[:, same], kept), (probe.at[:, cross], given)]
    moves += [
        (block.at[0, :, cross], stack.at[slots[i], :]) for i, block in enumerate((queries, keys, values))
    ]
    if stack.shape[0] > 4 * tokens:
        moves.append((probe.at[:, cross], stack.at[slots[3], :]))
    moves += [(block.at[0, :, same], own.at[i]) for i, block in enumerate((queries, keys, values))]
    copies = [
        pltpu.make_async_copy(source, target, sems.at[i]) for i, (source, target) in enumerate(moves)
    ]
    for copy in copies:
        copy.start()
    copies[0].wait()
    copies[1].wait()
    heads = gates.shape[1] // 2
    rows = []
    for kind in range(2):
        block = jnp.where(core == 0, gates[kind, heads:], gates[kind, :heads])
        for term in terms_of(block):
            rows += [term[:, begin : begin + width] for begin in range(0, tokens, width)]
    used = sum(row.shape[0] for row in rows)
    rows.append(jnp.zeros((GATE_ROWS - used, width), F32))
    stack[stack.shape[0] - GATE_ROWS :, :] = jnp.concatenate(rows, 0).astype(BF16)
    for copy in copies[2:]:
        copy.wait()


def received_gates(stack, tokens, heads):
    width = stack.shape[1]
    block = stack[stack.shape[0] - GATE_ROWS :, :].astype(F32)
    cuts = tokens // width
    out = []
    for kind in range(2):
        terms = []
        for term in range(3):
            begin = (kind * 3 + term) * cuts * heads
            terms.append(
                jnp.concatenate(
                    [block[begin + cut * heads : begin + (cut + 1) * heads] for cut in range(cuts)], 1
                )
            )
        out.append(terms[0] + terms[1] + terms[2])
    return out


def pack(place, with_probe, queries, keys, values, decay, beta, probe):
    tokens = queries.shape[1]
    width = queries.shape[2] // 2
    hbm_spec = pl.BlockSpec(memory_space=pltpu.HBM)
    vmem_spec = pl.BlockSpec(memory_space=pltpu.VMEM)
    half = jax.ShapeDtypeStruct((probe.shape[0], width), BF16)
    return pl.pallas_call(
        pack_kernel,
        grid_spec=pltpu.PrefetchScalarGridSpec(
            num_scalar_prefetch=1,
            grid=(),
            in_specs=[hbm_spec] * 6,
            out_specs=[vmem_spec] * 5,
            scratch_shapes=[pltpu.SemaphoreType.DMA((11,))],
        ),
        out_shape=[
            half,
            half,
            jax.ShapeDtypeStruct((3, tokens, width), BF16),
            jax.ShapeDtypeStruct(((4 if with_probe else 3) * tokens + GATE_ROWS, width), BF16),
            jax.ShapeDtypeStruct((2,) + decay.shape[1:], F32),
        ],
        compiler_params=pltpu.CompilerParams(vmem_limit_bytes=VMEM_BYTES),
        cost_estimate=cost(0.01),
        name="pack",
    )(place, *(in_hbm(block) for block in (queries, keys, values, decay, beta, probe)))


def prepare_kernel(side, tokens, place, stack, *refs):
    forth, back, back_low = refs[-3:]
    core = place[0]
    owner = core if side == 0 else 1 - core
    if side == 0:
        queries, keys = stack[0], stack[1]
    else:
        queries, keys = stack[:tokens], stack[tokens : 2 * tokens]
    width = queries.shape[1]
    spans, heads = tokens // SPAN, width // DK
    rows = lax.broadcasted_iota(jnp.int32, (SPAN, SPAN), 0)
    cols = lax.broadcasted_iota(jnp.int32, (SPAN, SPAN), 1)
    inclusive = rows >= cols
    strict = rows > cols
    diagonal = rows == cols
    items = [(span, head) for span in range(spans) for head in range(heads)]


    def cut(block, item):
        span, head = item
        return block[span * SPAN : (span + 1) * SPAN, head * DK : (head + 1) * DK]

    def cut_row(block, item):
        span, head = item
        return block[head : head + 1, span * SPAN : (span + 1) * SPAN]

    def column_of(row):
        return jnp.sum(jnp.where(diagonal, row, 0.0), 1, keepdims=True)

    def row_of(column):
        return jnp.sum(jnp.where(diagonal, column, 0.0), 0, keepdims=True)

    def lower_left(size):
        return (
            (rows // (2 * size) == cols // (2 * size))
            & ((rows // size) % 2 == 1)
            & ((cols // size) % 2 == 0)
        )

    if side == 0:
        gates = refs[0]
        decays, strengths = [
            jnp.where(core == 0, gates[kind, :heads], gates[kind, heads:]) for kind in range(2)
        ]
    else:
        decays, strengths = received_gates(stack, tokens, heads)
    decay_log = jnp.log(decays)
    identity = jnp.where(diagonal, 1.0, 0.0)

    def build(items):
        q = [unit(cut(queries, item)) for item in items]
        k = [unit(cut(keys, item)) for item in items]
        growth_log = [
            jnp.sum(jnp.where(inclusive, cut_row(decay_log, item), 0.0), 1, keepdims=True)
            for item in items
        ]
        strength_row = [cut_row(strengths, item) for item in items]
        inner = [dot_nt(jnp.concatenate([kk, qq], 0), kk) for kk, qq in zip(k, q)]
        ratios = [
            jnp.where(inclusive, jnp.exp(jnp.where(inclusive, log - row_of(log), 0.0)), 0.0)
            for log in growth_log
        ]
        coupling = [
            jnp.where(strict, column_of(row) * ratio * both[:SPAN], 0.0)
            for row, ratio, both in zip(strength_row, ratios, inner)
        ]
        mixing = [ratio * both[SPAN:] for ratio, both in zip(ratios, inner)]
        corner = lower_left(1)
        inverse = [identity - jnp.where(corner, block, 0.0) for block in coupling]
        size = 2
        while size < SPAN:
            corner = lower_left(size)
            narrow = [block.astype(BF16) for block in inverse]
            part = [
                dot(x, jnp.where(corner, a, 0.0).astype(BF16)) for x, a in zip(narrow, coupling)
            ]
            step_back = [dot(y.astype(BF16), x) for y, x in zip(part, narrow)]
            inverse = [x - z for x, z in zip(inverse, step_back)]
            size *= 2
        residual = [identity - x - fine_dot(a, x) for a, x in zip(coupling, inverse)]
        inverse = [x + dot(x.astype(BF16), e.astype(BF16)) for x, e in zip(inverse, residual)]
        scaled = [x * row for x, row in zip(inverse, strength_row)]
        growth = [jnp.exp(log) for log in growth_log]
        grown_keys = [g * kk.astype(F32) for g, kk in zip(growth, k)]
        grown_queries = [g * qq.astype(F32) for g, qq in zip(growth, q)]
        tails = [
            (jnp.exp(log[SPAN - 1 :] - log) * kk.astype(F32)).T for log, kk in zip(growth_log, k)
        ]
        upper = [
            fine_dot(jnp.concatenate([tail, mix], 0), b)
            for tail, mix, b in zip(tails, mixing, scaled)
        ]
        removed = [fine_dot(up, gk) for up, gk in zip(upper, grown_keys)]
        for item, g, up, rem, gq in zip(items, growth, upper, removed, grown_queries):
            span, head = item
            kept = jnp.where(diagonal, g[SPAN - 1 :], 0.0)
            whole = jnp.concatenate([jnp.concatenate([kept, gq], 0) - rem, up], 1)
            high, low = halves(whole.T)
            forth[owner, span, head] = whole.astype(BF16)
            back[owner, span, head] = high
            back_low[owner, span, head] = low

    for start in range(0, len(items), BATCH):
        build(items[start : start + BATCH])


BATCH = 8


def prepare(place, side, tokens, width, stack, others):
    heads = width // DK
    shape = (2, tokens // SPAN, heads, 2 * DK, 2 * DK)
    return kernel_call(
        functools.partial(prepare_kernel, side, tokens),
        "prepare",
        place,
        (stack,) + tuple(others),
        [(shape, BF16)] * 3,
        aliases={2 + index: index for index in range(3)} if side else {},
    )


def owned(place, blocks):
    mine, theirs = blocks
    first = place[0] == 0
    return jnp.where(first, mine, theirs), jnp.where(first, theirs, mine)


def row_block(place, block):
    if isinstance(block, int):
        return block
    chips, core = block
    if core == "same":
        core = place[0]
    elif core == "other":
        core = 1 - place[0]
    return 2 * lax.bitwise_xor(place[1], chips) + core


def columns_of(place, block, width):
    return pl.ds(pl.multiple_of(row_block(place, block) * width, width), width)


def positions_of(owner, tokens):
    return pl.ds(pl.multiple_of(owner * tokens, tokens), tokens)


def load_piece(ref, rows):
    return ref[:rows] if ref.shape[0] < 3 * rows else ref[3 * rows : 4 * rows]


def read_kernel(with_state, blocks, place, mine, theirs, own, stack, back, low, *refs):
    count = len(blocks)
    pieces, refs = refs[:count], refs[count:]
    if with_state:
        (first, *refs) = refs
    (total, kept, given, last, read) = refs
    tokens, width = own.shape[1:]
    spans, heads = back.shape[1:3]
    core = place[0]
    values = owned(place, (own[2], stack[2 * tokens : 3 * tokens]))
    zero = jnp.zeros((DK, DK), F32)
    states = [first[head] if with_state else zero for head in range(heads)]
    for half in range(2):
        for span in range(spans):
            for head in range(heads):
                positions = slice(span * SPAN, (span + 1) * SPAN)
                columns = slice(head * DK, (head + 1) * DK)
                block = values[half][positions, columns].T
                x_high, x_low = halves(states[head])
                left = jnp.concatenate([x_high, block], 1)
                rest = jnp.concatenate([x_low, jnp.zeros_like(block)], 1)
                both = dot(jnp.concatenate([left, rest], 0), back[half, span, head])
                result = both[:DK] + both[DK:] + dot(left, low[half, span, head])
                states[head] = result[:, :DK]
                read[half, positions, columns] = result[:, DK:].T.astype(BF16)
    for head in range(heads):
        last[head] = states[head]
    kept[...] = read[core]
    given[...] = read[1 - core]
    add_products(place, blocks, mine, theirs, pieces, total, None)


def paired(blocks):
    return not isinstance(blocks[0], int) and blocks[0][0] == blocks[1][0]


def add_products(place, blocks, mine, theirs, pieces, result, total):
    tokens = mine.shape[0]
    rows = mine.shape[1] // 8
    core = place[0]
    probe = [load_piece(piece, rows) for piece in pieces]
    for source, owner in ((mine, core), (theirs, 1 - core)):
        positions = positions_of(owner, tokens)
        begin = 0
        part = None if total is None else total[positions, :]
        if paired(blocks):
            chip = lax.bitwise_xor(place[1], blocks[0][0])
            columns = pl.ds(pl.multiple_of(chip * 2 * rows, 2 * rows), 2 * rows)
            product = dot(source[:, columns], jnp.concatenate(owned(place, probe[:2]), 0))
            part = product if part is None else part + product
            begin = 2
        for block, piece in zip(blocks[begin:], probe[begin:]):
            product = dot(source[:, columns_of(place, block, rows)], piece)
            part = product if part is None else part + product
        result[positions, :] = part.astype(result.dtype)


def read_values(place, mine, theirs, own, stack, maps, blocks, pieces, entry):
    tokens, width = own.shape[1:]
    heads = width // DK
    extra = () if entry is None else (entry,)
    return kernel_call(
        functools.partial(read_kernel, entry is not None, tuple(blocks)),
        "read_values",
        place,
        (mine, theirs, own, stack, maps[1], maps[2], *pieces, *extra),
        [
            ((2 * tokens, width), F32),
            ((tokens, width), BF16),
            ((tokens, width), BF16),
            ((heads, DK, DK), F32),
        ],
        scratch=[pltpu.VMEM((2, tokens, width), BF16)],
    )


def recur_kernel(weighting, with_state, blocks, chips, lists, place, mine, theirs, total, forth, back, read, *refs):
    count = len(blocks)
    pieces, refs = refs[:count], refs[count:]
    if with_state:
        (first, final, *refs) = refs
    (grads, last, start, *refs) = refs
    width = total.shape[1]
    shares, (sums, up) = refs[: len(lists)], refs[len(lists) :]
    tokens = mine.shape[0]
    spans, heads = forth.shape[1:3]
    add_products(place, blocks, mine, theirs, pieces, sums, total)
    zero = jnp.zeros((DK, DK), F32)
    states = [first[head] if with_state else zero for head in range(heads)]
    steps = [(half, span) for half in range(2) for span in range(spans)]
    for half, span in steps:
        begin = half * tokens + span * SPAN
        for head in range(heads):
            block = sums[begin : begin + SPAN, head * DK : (head + 1) * DK].T.astype(BF16)
            left = jnp.concatenate([states[head].astype(BF16), block], 1)
            result = dot(left, back[half, span, head])
            states[head] = result[:, :DK]
            up[half, span, head] = (weighting * result[:, DK:]).astype(BF16)
    for head in range(heads):
        last[head] = states[head]
    states = [final[head] if with_state else zero for head in range(heads)]
    for half, span in reversed(steps):
        begin = half * tokens + span * SPAN
        for head in range(heads):
            left = jnp.concatenate([states[head].astype(BF16), up[half, span, head]], 1)
            result = dot(left, forth[half, span, head])
            states[head] = result[:, :DK]
            row = begin // width * width + head * DK
            grads[row : row + DK, begin % width : begin % width + SPAN] = result[:, DK:].astype(BF16)
    grads[2 * tokens :, :] = read[...]
    for head in range(heads):
        start[head] = states[head]
    if lists:
        put_products(place, chips, lists, mine, theirs, grads, shares)


def grads_of(grads, owner, tokens):
    width = grads.shape[1]
    block = grads[positions_of(owner, tokens), :]
    return jnp.concatenate([block[i : i + width] for i in range(0, tokens, width)], 1)


def put_products(place, chips, lists, mine, theirs, grads, outs):
    tokens, width = mine.shape
    if chips is None:
        columns = pl.ds(0, width)
    else:
        columns = pl.ds(pl.multiple_of(lax.bitwise_xor(place[1], chips) * 4 * ROWS, 4 * ROWS), 4 * ROWS)
    core = place[0]
    part = dot(grads_of(grads, core, tokens), mine[:, columns])
    part += dot(grads_of(grads, 1 - core, tokens), theirs[:, columns])
    part = part.T
    for out, indices in zip(outs, lists):
        for slot, index in enumerate(indices):
            out[slot] = part[index * ROWS : (index + 1) * ROWS].astype(out.dtype)


def recur(weighting, place, mine, theirs, total, maps, read, blocks, pieces, chips, lists, states):
    tokens = mine.shape[0]
    width = total.shape[1]
    spans, heads = maps[0].shape[1:3]
    extra = () if states is None else states
    return kernel_call(
        functools.partial(
            recur_kernel, weighting, states is not None, tuple(blocks), chips, lists
        ),
        "recur",
        place,
        (mine, theirs, total, maps[0], maps[1], read, *pieces, *extra),
        [((3 * tokens, width), BF16), ((heads, DK, DK), F32), ((heads, DK, DK), F32)]
        + [((len(part), ROWS, width), BF16) for part in lists],
        scratch=[
            pltpu.VMEM((2 * tokens, width), F32),
            pltpu.VMEM((2, spans, heads, DK, SPAN), BF16),
        ],
    )


ROWS = 256


def curvature_kernel(jobs, place, mine, theirs, grads, *outs):
    begin = 0
    for chips, lists in jobs:
        put_products(place, chips, lists, mine, theirs, grads, outs[begin : begin + len(lists)])
        begin += len(lists)


def curvature(place, mine, theirs, grads, jobs, types):
    width = grads.shape[1]
    lengths = [len(part) for chips, lists in jobs for part in lists]
    return kernel_call(
        functools.partial(curvature_kernel, jobs),
        "curvature",
        place,
        (mine, theirs, grads),
        [((length, ROWS, width), kind) for length, kind in zip(lengths, types)],
    )


def keep_kernel(place, mine, theirs, grads, keep_x, keep_y):
    for chips, half, out in ((1, 1, keep_x), (2, 0, keep_y)):
        for block in range(2):
            columns = half_block(place, chips, block, half)
            out[block] = products(place, mine, theirs, grads, columns)


def half_block(place, chips, block, half):
    index = 2 * (2 * lax.bitwise_xor(place[1], chips) + block) + half
    return pl.ds(pl.multiple_of(index * ROWS, ROWS), ROWS)


def products(place, mine, theirs, grads, columns):
    tokens = mine.shape[0]
    core = place[0]
    part = dot(grads_of(grads, core, tokens), mine[:, columns])
    part += dot(grads_of(grads, 1 - core, tokens), theirs[:, columns])
    return part.T


def keep(place, mine, theirs, grads):
    shape = (2, ROWS, grads.shape[1])
    return kernel_call(keep_kernel, "keep", place, (mine, theirs, grads), [(shape, F32)] * 2)


def near_kernel(place, mine, theirs, grads, grads_other, read, near_x, near_y, own, mixed):
    core = place[0]
    tokens, width = read.shape
    join(place, read[...], grads_other[2 * tokens :, :], mixed)
    jobs = (
        (half_block(place, 1, core, 0), near_x),
        (half_block(place, 2, core, 1), near_y),
        (pl.ds(pl.multiple_of((2 * place[1] + core) * 2 * ROWS, 2 * ROWS), 2 * ROWS), own),
    )
    for columns, out in jobs:
        for source, owner in ((grads, core), (grads_other, 1 - core)):
            part = products(place, mine, theirs, source, columns)
            out[:, positions_of(owner, width)] = part.astype(out.dtype)


def near(place, mine, theirs, grads, grads_other, read):
    rows, width = read.shape
    return kernel_call(
        near_kernel,
        "near",
        place,
        (mine, theirs, grads, grads_other, read),
        [
            ((ROWS, 2 * width), BF16),
            ((ROWS, 2 * width), BF16),
            ((2 * ROWS, 2 * width), F32),
            ((rows, 2 * width), BF16),
        ],
    )


def join(place, same, cross, whole):
    width = same.shape[1]
    whole[:, positions_of(place[0], width)] = same
    whole[:, positions_of(1 - place[0], width)] = cross


def relay_kernel(place, far_x, far_y, keep_x, keep_y, after, *outs):
    core = place[0]
    for index, (far, keep) in enumerate(((far_x, keep_y), (far_y, keep_x))):
        for which, owner in enumerate((core, 1 - core)):
            outs[2 * index + which][...] = (keep[owner] + far[owner].astype(F32)).astype(BF16)


def relay(place, far_x, far_y, keep_x, keep_y, after):
    shape = keep_x.shape[1:]
    operands = (far_x, far_y, keep_x, keep_y, after)
    return kernel_call(relay_kernel, "relay", place, operands, [(shape, BF16)] * 4)


def finish_kernel(place, own, near_x, near_y, top_same, low_same, top_cross, low_cross, whole):
    core = place[0]
    width = top_same.shape[1]
    for owner, top, low in ((core, top_same, low_same), (1 - core, top_cross, low_cross)):
        columns = positions_of(owner, width)
        for rows, first, second in ((slice(0, ROWS), near_x, top), (slice(ROWS, 2 * ROWS), near_y, low)):
            part = first[:, columns].astype(F32) + second[...].astype(F32)
            whole[rows, columns] = own[rows, columns] + part


def finish(place, *parts):
    return kernel_call(finish_kernel, "finish", place, parts, [(parts[0].shape, F32)])[0]


def join_kernel(place, same, cross, whole):
    join(place, same[...], cross[...], whole)


def local(square, dp_size, ctx_size, queries, keys, values, decay, beta, inputs, probe):
    tokens = queries.shape[1]
    width = queries.shape[2] // 2
    weighting = math.sqrt(D) / (dp_size * ctx_size * tokens)
    ctx = lax.axis_index("ctx")
    chip = lax.axis_index("dp")
    core = lax.rem(ctx, 2)
    groups = ctx_size // 2
    partner = [(index, index ^ 1) for index in range(ctx_size)]
    mine = inputs[0]
    place = jnp.stack([core, chip])

    def swap(block):
        return lax.ppermute(block, "ctx", partner)

    def send(block, chips, cores):
        pairs = [
            (2 * index + which, 2 * (index ^ chips) + (which ^ cores))
            for index in range(dp_size)
            for which in range(2)
        ]
        return lax.ppermute(block, GROUP, pairs)

    def part(block, index):
        return lax.dynamic_slice_in_dim(block, index * width, width, 1)

    kept, given, own, stack, gates = pack(place, square, queries, keys, values, decay, beta, probe)
    if square:
        stack, mine = lax.optimization_barrier((stack, mine))
        stack = swap(stack)
        theirs = swap(mine)
        x_one = send(kept, 1, 0)
        y_one = send(given, 2, 1)
        x_two = send(given, 1, 1)
        maps = prepare(place, 0, tokens, width, own, (gates,))
        late, *maps = lax.optimization_barrier((kept, *maps))
        y_two = send(late, 2, 0)
        x_one, y_one, *maps = lax.optimization_barrier((x_one, y_one, *maps))
        far_one = send(x_one, 2, 0)
        far_two = send(y_one, 1, 0)
        maps = prepare(place, 1, tokens, width, stack, maps)
        pieces = [kept, stack, x_one, y_one, x_two, y_two, far_one, far_two]
        places = [
            (0, "same"),
            (0, "other"),
            (1, "same"),
            (2, "other"),
            (1, "other"),
            (2, "same"),
            (3, "same"),
            (3, "other"),
        ]
    else:
        stack = swap(stack)
        theirs = swap(mine)
        maps = prepare(place, 0, tokens, width, own, (gates,))
        maps = prepare(place, 1, tokens, width, stack, maps)
        gathered = part(lax.all_gather(probe, GROUP, axis=0, tiled=True), core)
        places = list(range(8))
        rows = D // len(places)
        pieces = [gathered[index * rows : (index + 1) * rows] for index in places]
    def shift(block, by):
        pairs = [
            (index, index + 2 * by)
            for index in range(ctx_size)
            if 0 <= index + 2 * by < ctx_size
        ]
        return lax.ppermute(block, "ctx", pairs)

    entry = None
    if groups > 1:
        entry = jnp.zeros((width // DK, DK, DK), F32)
    read = functools.partial(
        read_values,
        place,
        mine,
        theirs,
        own,
        stack,
        maps,
        places[:6],
        pieces[:6],
    )
    for _ in range(groups - 1):
        entry = shift(read(entry)[3], 1)
    total, read_kept, read_given, unused = read(entry)
    lists = ((0, 2), (1, 3)) if square else ()
    run = functools.partial(
        recur,
        weighting,
        place,
        mine,
        theirs,
        total,
        maps,
        read_given,
        places[6:],
        pieces[6:],
        3,
        lists,
    )
    states = None
    if groups > 1:
        states = (jnp.zeros((width // DK, DK, DK), F32),) * 2
        for _ in range(groups - 1):
            states = (shift(run(states)[1], 1), states[1])
        for _ in range(groups - 1):
            states = (states[0], shift(run(states)[2], -1))
    grads, unused, unused, *shares = run(states)
    build = functools.partial(curvature, place, mine, theirs, grads)
    if not square:
        everything = build(((None, (tuple(range(D // ROWS)),)),), [F32])[0]
        flat = everything.reshape(D, width)
        zero = jnp.zeros_like(flat)
        both = jnp.where(
            core == 0, jnp.concatenate([flat, zero], 1), jnp.concatenate([zero, flat], 1)
        )
        read_swapped = swap(read_given)
        mixed = kernel_call(
            join_kernel, "join", place, (read_kept, read_swapped), [((tokens, 2 * width), BF16)]
        )[0]
        return mixed[None], lax.psum_scatter(both, GROUP, scatter_dimension=0, tiled=True)

    far_x = send(shares[0], 1, 0)
    far_y = send(shares[1], 2, 0)
    grads_other = swap(grads)
    keep_x, keep_y = keep(place, mine, theirs, grads)
    near_x, near_y, rest, mixed = near(place, mine, theirs, grads, grads_other, read_kept)
    after = near_x
    near_x = send(near_x, 1, 0)
    near_y = send(near_y, 2, 0)
    top_same, top_cross, low_same, low_cross = relay(place, far_x, far_y, keep_x, keep_y, after)
    top_same = send(top_same, 2, 0)
    low_same = send(low_same, 1, 0)
    near_x, near_y, top_cross, low_cross = lax.optimization_barrier(
        (near_x, near_y, top_cross, low_cross)
    )
    top_cross = send(top_cross, 2, 1)
    low_cross = send(low_cross, 1, 1)
    result = finish(place, rest, near_x, near_y, top_same, low_same, top_cross, low_cross)
    return mixed[None], result


def solution(mesh):
    dp_size, ctx_size = mesh.shape["dp"], mesh.shape["ctx"]
    square = dp_size == 4 and ctx_size == 2
    return jax.shard_map(
        functools.partial(local, square, dp_size, ctx_size),
        mesh=mesh,
        in_specs=(
            P("dp", "ctx", "head"),
            P("dp", "ctx", "head"),
            P("dp", "ctx", "head"),
            P("dp", "head", "ctx"),
            P("dp", "head", "ctx"),
            P("dp", "ctx", None),
            P(("dp", "ctx"), "head"),
        ),
        out_specs=(P("dp", "ctx", "head"), P(("dp", "ctx"), "head")),
        check_vma=False,
    )
```

```python
import functools
import math

import jax
import jax.numpy as jnp
from jax import lax
from jax.experimental import pallas as pl
from jax.experimental.pallas import tpu as pltpu
from jax.sharding import PartitionSpec as P

D = 4096
DK = 128
SPAN = 128
EPSILON = 1e-06
GROUP = ("dp", "ctx")
BF16 = jnp.bfloat16
F32 = jnp.float32
VMEM_BYTES = 24 * 1024 * 1024


def cost(us):
    return pl.CostEstimate(flops=int(us * 1.1e9), bytes_accessed=int(us * 3.0e6), transcendentals=0)


def in_hbm(block):
    return pltpu.with_memory_space_constraint(block, pltpu.HBM)


def in_vmem(block):
    return pltpu.with_memory_space_constraint(block, pltpu.VMEM)


def kernel_call(kernel, name, place, operands, outs, scratch=(), aliases=None, far=()):
    vmem_spec = pl.BlockSpec(memory_space=pltpu.VMEM)
    return pl.pallas_call(
        kernel,
        grid_spec=pltpu.PrefetchScalarGridSpec(
            num_scalar_prefetch=1,
            grid=(),
            in_specs=[pl.BlockSpec(memory_space=pltpu.HBM)] * len(far) + [vmem_spec] * len(operands),
            out_specs=[vmem_spec] * len(outs),
            scratch_shapes=list(scratch),
        ),
        out_shape=[jax.ShapeDtypeStruct(shape, kind) for shape, kind in outs],
        input_output_aliases=aliases or {},
        compiler_params=pltpu.CompilerParams(vmem_limit_bytes=VMEM_BYTES),
        cost_estimate=cost(0.01),
        name=name,
    )(place, *(in_hbm(block) for block in far), *(in_vmem(block) for block in operands))


def dot(left, right):
    return jnp.dot(left, right, preferred_element_type=F32)


def dot_nt(left, right):
    return lax.dot_general(left, right, (((1,), (1,)), ((), ())), preferred_element_type=F32)


def halves(block):
    high = block.astype(BF16)
    return high, (block - high.astype(F32)).astype(BF16)


def fine_dot(left, right):
    left_high, left_low = halves(left)
    right_high, right_low = halves(right)
    wide = jnp.concatenate([right_high, right_low], 1)
    both = dot(jnp.concatenate([left_high, left_low], 1), jnp.concatenate([wide, wide], 0))
    width = right.shape[1]
    return both[:, :width] + both[:, width:]


def unit(block):
    block = block.astype(F32)
    return (block * lax.rsqrt(jnp.sum(block * block, -1, keepdims=True) + EPSILON)).astype(BF16)


GATE_ROWS = 32


def terms_of(block):
    terms = []
    for _ in range(3):
        term = block.astype(BF16)
        terms.append(term.astype(F32))
        block = block - terms[-1]
    return terms


def pack_kernel(place, queries, keys, values, decay, beta, probe, kept, given, own, stack, gates, sems):
    core = place[0]
    tokens, width = own.shape[1:]
    same = pl.ds(pl.multiple_of(core * width, width), width)
    cross = pl.ds(pl.multiple_of((1 - core) * width, width), width)
    slots = [pl.ds(i * tokens, tokens) for i in range(4)]
    moves = [(decay.at[0], gates.at[0]), (beta.at[0], gates.at[1])]
    moves += [(probe.at[:, same], kept), (probe.at[:, cross], given)]
    moves += [
        (block.at[0, :, cross], stack.at[slots[i], :]) for i, block in enumerate((queries, keys, values))
    ]
    if stack.shape[0] > 4 * tokens:
        moves.append((probe.at[:, cross], stack.at[slots[3], :]))
    moves += [(block.at[0, :, same], own.at[i]) for i, block in enumerate((queries, keys, values))]
    copies = [
        pltpu.make_async_copy(source, target, sems.at[i]) for i, (source, target) in enumerate(moves)
    ]
    for copy in copies:
        copy.start()
    copies[0].wait()
    copies[1].wait()
    heads = gates.shape[1] // 2
    rows = []
    for kind in range(2):
        block = jnp.where(core == 0, gates[kind, heads:], gates[kind, :heads])
        for term in terms_of(block):
            rows += [term[:, begin : begin + width] for begin in range(0, tokens, width)]
    used = sum(row.shape[0] for row in rows)
    rows.append(jnp.zeros((GATE_ROWS - used, width), F32))
    stack[stack.shape[0] - GATE_ROWS :, :] = jnp.concatenate(rows, 0).astype(BF16)
    for copy in copies[2:]:
        copy.wait()


def received_gates(stack, tokens, heads):
    width = stack.shape[1]
    block = stack[stack.shape[0] - GATE_ROWS :, :].astype(F32)
    cuts = tokens // width
    out = []
    for kind in range(2):
        terms = []
        for term in range(3):
            begin = (kind * 3 + term) * cuts * heads
            terms.append(
                jnp.concatenate(
                    [block[begin + cut * heads : begin + (cut + 1) * heads] for cut in range(cuts)], 1
                )
            )
        out.append(terms[0] + terms[1] + terms[2])
    return out


def pack(place, with_probe, queries, keys, values, decay, beta, probe):
    tokens = queries.shape[1]
    width = queries.shape[2] // 2
    hbm_spec = pl.BlockSpec(memory_space=pltpu.HBM)
    vmem_spec = pl.BlockSpec(memory_space=pltpu.VMEM)
    half = jax.ShapeDtypeStruct((probe.shape[0], width), BF16)
    return pl.pallas_call(
        pack_kernel,
        grid_spec=pltpu.PrefetchScalarGridSpec(
            num_scalar_prefetch=1,
            grid=(),
            in_specs=[hbm_spec] * 6,
            out_specs=[vmem_spec] * 5,
            scratch_shapes=[pltpu.SemaphoreType.DMA((11,))],
        ),
        out_shape=[
            half,
            half,
            jax.ShapeDtypeStruct((3, tokens, width), BF16),
            jax.ShapeDtypeStruct(((4 if with_probe else 3) * tokens + GATE_ROWS, width), BF16),
            jax.ShapeDtypeStruct((2,) + decay.shape[1:], F32),
        ],
        compiler_params=pltpu.CompilerParams(vmem_limit_bytes=VMEM_BYTES),
        cost_estimate=cost(0.01),
        name="pack",
    )(place, *(in_hbm(block) for block in (queries, keys, values, decay, beta, probe)))


def prepare_kernel(side, tokens, place, stack, *refs):
    forth, back, back_low = refs[-3:]
    core = place[0]
    owner = core if side == 0 else 1 - core
    if side == 0:
        queries, keys = stack[0], stack[1]
    else:
        queries, keys = stack[:tokens], stack[tokens : 2 * tokens]
    width = queries.shape[1]
    spans, heads = tokens // SPAN, width // DK
    rows = lax.broadcasted_iota(jnp.int32, (SPAN, SPAN), 0)
    cols = lax.broadcasted_iota(jnp.int32, (SPAN, SPAN), 1)
    inclusive = rows >= cols
    strict = rows > cols
    diagonal = rows == cols
    items = [(span, head) for span in range(spans) for head in range(heads)]


    def cut(block, item):
        span, head = item
        return block[span * SPAN : (span + 1) * SPAN, head * DK : (head + 1) * DK]

    def cut_row(block, item):
        span, head = item
        return block[head : head + 1, span * SPAN : (span + 1) * SPAN]

    def column_of(row):
        return jnp.sum(jnp.where(diagonal, row, 0.0), 1, keepdims=True)

    def row_of(column):
        return jnp.sum(jnp.where(diagonal, column, 0.0), 0, keepdims=True)

    def lower_left(size):
        return (
            (rows // (2 * size) == cols // (2 * size))
            & ((rows // size) % 2 == 1)
            & ((cols // size) % 2 == 0)
        )

    if side == 0:
        gates = refs[0]
        decays, strengths = [
            jnp.where(core == 0, gates[kind, :heads], gates[kind, heads:]) for kind in range(2)
        ]
    else:
        decays, strengths = received_gates(stack, tokens, heads)
    decay_log = jnp.log(decays)
    identity = jnp.where(diagonal, 1.0, 0.0)

    def build(items):
        q = [unit(cut(queries, item)) for item in items]
        k = [unit(cut(keys, item)) for item in items]
        growth_log = [
            jnp.sum(jnp.where(inclusive, cut_row(decay_log, item), 0.0), 1, keepdims=True)
            for item in items
        ]
        strength_row = [cut_row(strengths, item) for item in items]
        inner = [dot_nt(jnp.concatenate([kk, qq], 0), kk) for kk, qq in zip(k, q)]
        ratios = [
            jnp.where(inclusive, jnp.exp(jnp.where(inclusive, log - row_of(log), 0.0)), 0.0)
            for log in growth_log
        ]
        coupling = [
            jnp.where(strict, column_of(row) * ratio * both[:SPAN], 0.0)
            for row, ratio, both in zip(strength_row, ratios, inner)
        ]
        mixing = [ratio * both[SPAN:] for ratio, both in zip(ratios, inner)]
        corner = lower_left(1)
        inverse = [identity - jnp.where(corner, block, 0.0) for block in coupling]
        size = 2
        while size < SPAN:
            corner = lower_left(size)
            narrow = [block.astype(BF16) for block in inverse]
            part = [
                dot(x, jnp.where(corner, a, 0.0).astype(BF16)) for x, a in zip(narrow, coupling)
            ]
            step_back = [dot(y.astype(BF16), x) for y, x in zip(part, narrow)]
            inverse = [x - z for x, z in zip(inverse, step_back)]
            size *= 2
        residual = [identity - x - fine_dot(a, x) for a, x in zip(coupling, inverse)]
        inverse = [x + dot(x.astype(BF16), e.astype(BF16)) for x, e in zip(inverse, residual)]
        scaled = [x * row for x, row in zip(inverse, strength_row)]
        growth = [jnp.exp(log) for log in growth_log]
        grown_keys = [g * kk.astype(F32) for g, kk in zip(growth, k)]
        grown_queries = [g * qq.astype(F32) for g, qq in zip(growth, q)]
        tails = [
            (jnp.exp(log[SPAN - 1 :] - log) * kk.astype(F32)).T for log, kk in zip(growth_log, k)
        ]
        upper = [
            fine_dot(jnp.concatenate([tail, mix], 0), b)
            for tail, mix, b in zip(tails, mixing, scaled)
        ]
        removed = [fine_dot(up, gk) for up, gk in zip(upper, grown_keys)]
        for item, g, up, rem, gq in zip(items, growth, upper, removed, grown_queries):
            span, head = item
            kept = jnp.where(diagonal, g[SPAN - 1 :], 0.0)
            whole = jnp.concatenate([jnp.concatenate([kept, gq], 0) - rem, up], 1)
            high, low = halves(whole.T)
            forth[owner, span, head] = whole.astype(BF16)
            back[owner, span, head] = high
            back_low[owner, span, head] = low

    for start in range(0, len(items), BATCH):
        build(items[start : start + BATCH])


BATCH = 8


def prepare(place, side, tokens, width, stack, others):
    heads = width // DK
    shape = (2, tokens // SPAN, heads, 2 * DK, 2 * DK)
    return kernel_call(
        functools.partial(prepare_kernel, side, tokens),
        "prepare",
        place,
        (stack,) + tuple(others),
        [(shape, BF16)] * 3,
        aliases={2 + index: index for index in range(3)} if side else {},
    )


def owned(place, blocks):
    mine, theirs = blocks
    first = place[0] == 0
    return jnp.where(first, mine, theirs), jnp.where(first, theirs, mine)


def row_block(place, block):
    if isinstance(block, int):
        return block
    chips, core = block
    if core == "same":
        core = place[0]
    elif core == "other":
        core = 1 - place[0]
    return 2 * lax.bitwise_xor(place[1], chips) + core


def columns_of(place, block, width):
    return pl.ds(pl.multiple_of(row_block(place, block) * width, width), width)


def positions_of(owner, tokens):
    return pl.ds(pl.multiple_of(owner * tokens, tokens), tokens)


def load_piece(ref, rows):
    return ref[:rows] if ref.shape[0] < 3 * rows else ref[3 * rows : 4 * rows]


def read_kernel(with_state, blocks, place, mine, theirs, own, stack, back, low, *refs):
    count = len(blocks)
    pieces, refs = refs[:count], refs[count:]
    if with_state:
        (first, *refs) = refs
    (total, kept, given, last, read) = refs
    tokens, width = own.shape[1:]
    spans, heads = back.shape[1:3]
    core = place[0]
    values = owned(place, (own[2], stack[2 * tokens : 3 * tokens]))
    zero = jnp.zeros((DK, DK), F32)
    states = [first[head] if with_state else zero for head in range(heads)]
    for half in range(2):
        for span in range(spans):
            for head in range(heads):
                positions = slice(span * SPAN, (span + 1) * SPAN)
                columns = slice(head * DK, (head + 1) * DK)
                block = values[half][positions, columns].T
                x_high, x_low = halves(states[head])
                left = jnp.concatenate([x_high, block], 1)
                rest = jnp.concatenate([x_low, jnp.zeros_like(block)], 1)
                both = dot(jnp.concatenate([left, rest], 0), back[half, span, head])
                result = both[:DK] + both[DK:] + dot(left, low[half, span, head])
                states[head] = result[:, :DK]
                read[half, positions, columns] = result[:, DK:].T.astype(BF16)
    for head in range(heads):
        last[head] = states[head]
    kept[...] = read[core]
    given[...] = read[1 - core]
    add_products(place, blocks, mine, theirs, pieces, total, None)


def paired(blocks):
    return not isinstance(blocks[0], int) and blocks[0][0] == blocks[1][0]


def add_products(place, blocks, mine, theirs, pieces, result, total):
    tokens = mine.shape[0]
    rows = mine.shape[1] // 8
    core = place[0]
    probe = [load_piece(piece, rows) for piece in pieces]
    for source, owner in ((mine, core), (theirs, 1 - core)):
        positions = positions_of(owner, tokens)
        begin = 0
        part = None if total is None else total[positions, :]
        if paired(blocks):
            chip = lax.bitwise_xor(place[1], blocks[0][0])
            columns = pl.ds(pl.multiple_of(chip * 2 * rows, 2 * rows), 2 * rows)
            product = dot(source[:, columns], jnp.concatenate(owned(place, probe[:2]), 0))
            part = product if part is None else part + product
            begin = 2
        for block, piece in zip(blocks[begin:], probe[begin:]):
            product = dot(source[:, columns_of(place, block, rows)], piece)
            part = product if part is None else part + product
        result[positions, :] = part.astype(result.dtype)


def read_values(place, mine, theirs, own, stack, maps, blocks, pieces, entry):
    tokens, width = own.shape[1:]
    heads = width // DK
    extra = () if entry is None else (entry,)
    return kernel_call(
        functools.partial(read_kernel, entry is not None, tuple(blocks)),
        "read_values",
        place,
        (mine, theirs, own, stack, maps[1], maps[2], *pieces, *extra),
        [
            ((2 * tokens, width), F32),
            ((tokens, width), BF16),
            ((tokens, width), BF16),
            ((heads, DK, DK), F32),
        ],
        scratch=[pltpu.VMEM((2, tokens, width), BF16)],
    )


def recur_kernel(weighting, with_state, blocks, chips, lists, place, mine, theirs, total, forth, back, read, *refs):
    count = len(blocks)
    pieces, refs = refs[:count], refs[count:]
    if with_state:
        (first, final, *refs) = refs
    (grads, last, start, *refs) = refs
    width = total.shape[1]
    shares, (sums, up) = refs[: len(lists)], refs[len(lists) :]
    tokens = mine.shape[0]
    spans, heads = forth.shape[1:3]
    add_products(place, blocks, mine, theirs, pieces, sums, total)
    zero = jnp.zeros((DK, DK), F32)
    states = [first[head] if with_state else zero for head in range(heads)]
    steps = [(half, span) for half in range(2) for span in range(spans)]
    for half, span in steps:
        begin = half * tokens + span * SPAN
        for head in range(heads):
            block = sums[begin : begin + SPAN, head * DK : (head + 1) * DK].T.astype(BF16)
            left = jnp.concatenate([states[head].astype(BF16), block], 1)
            result = dot(left, back[half, span, head])
            states[head] = result[:, :DK]
            up[half, span, head] = (weighting * result[:, DK:]).astype(BF16)
    for head in range(heads):
        last[head] = states[head]
    states = [final[head] if with_state else zero for head in range(heads)]
    for half, span in reversed(steps):
        begin = half * tokens + span * SPAN
        for head in range(heads):
            left = jnp.concatenate([states[head].astype(BF16), up[half, span, head]], 1)
            result = dot(left, forth[half, span, head])
            states[head] = result[:, :DK]
            row = begin // width * width + head * DK
            grads[row : row + DK, begin % width : begin % width + SPAN] = result[:, DK:].astype(BF16)
    grads[2 * tokens :, :] = read[...]
    for head in range(heads):
        start[head] = states[head]
    if lists:
        put_products(place, chips, lists, mine, theirs, grads, shares)


def grads_of(grads, owner, tokens):
    width = grads.shape[1]
    block = grads[positions_of(owner, tokens), :]
    return jnp.concatenate([block[i : i + width] for i in range(0, tokens, width)], 1)


def put_products(place, chips, lists, mine, theirs, grads, outs):
    tokens, width = mine.shape
    if chips is None:
        columns = pl.ds(0, width)
    else:
        columns = pl.ds(pl.multiple_of(lax.bitwise_xor(place[1], chips) * 4 * ROWS, 4 * ROWS), 4 * ROWS)
    core = place[0]
    part = dot(grads_of(grads, core, tokens), mine[:, columns])
    part += dot(grads_of(grads, 1 - core, tokens), theirs[:, columns])
    part = part.T
    for out, indices in zip(outs, lists):
        for slot, index in enumerate(indices):
            out[slot] = part[index * ROWS : (index + 1) * ROWS].astype(out.dtype)


def recur(weighting, place, mine, theirs, total, maps, read, blocks, pieces, chips, lists, states):
    tokens = mine.shape[0]
    width = total.shape[1]
    spans, heads = maps[0].shape[1:3]
    extra = () if states is None else states
    return kernel_call(
        functools.partial(
            recur_kernel, weighting, states is not None, tuple(blocks), chips, lists
        ),
        "recur",
        place,
        (mine, theirs, total, maps[0], maps[1], read, *pieces, *extra),
        [((3 * tokens, width), BF16), ((heads, DK, DK), F32), ((heads, DK, DK), F32)]
        + [((len(part), ROWS, width), BF16) for part in lists],
        scratch=[
            pltpu.VMEM((2 * tokens, width), F32),
            pltpu.VMEM((2, spans, heads, DK, SPAN), BF16),
        ],
    )


ROWS = 256


def curvature_kernel(jobs, place, mine, theirs, grads, *outs):
    begin = 0
    for chips, lists in jobs:
        put_products(place, chips, lists, mine, theirs, grads, outs[begin : begin + len(lists)])
        begin += len(lists)


def curvature(place, mine, theirs, grads, jobs, types):
    width = grads.shape[1]
    lengths = [len(part) for chips, lists in jobs for part in lists]
    return kernel_call(
        functools.partial(curvature_kernel, jobs),
        "curvature",
        place,
        (mine, theirs, grads),
        [((length, ROWS, width), kind) for length, kind in zip(lengths, types)],
    )


def keep_kernel(place, mine, theirs, grads, keep_x, keep_y):
    for chips, half, out in ((1, 1, keep_x), (2, 0, keep_y)):
        for block in range(2):
            columns = half_block(place, chips, block, half)
            out[block] = products(place, mine, theirs, grads, columns)


def half_block(place, chips, block, half):
    index = 2 * (2 * lax.bitwise_xor(place[1], chips) + block) + half
    return pl.ds(pl.multiple_of(index * ROWS, ROWS), ROWS)


def products(place, mine, theirs, grads, columns):
    tokens = mine.shape[0]
    core = place[0]
    part = dot(grads_of(grads, core, tokens), mine[:, columns])
    part += dot(grads_of(grads, 1 - core, tokens), theirs[:, columns])
    return part.T


def keep(place, mine, theirs, grads):
    shape = (2, ROWS, grads.shape[1])
    return kernel_call(keep_kernel, "keep", place, (mine, theirs, grads), [(shape, F32)] * 2)


def near_kernel(place, mine, theirs, grads, grads_other, read, near_x, near_y, own, mixed):
    core = place[0]
    tokens, width = read.shape
    join(place, read[...], grads_other[2 * tokens :, :], mixed)
    jobs = (
        (half_block(place, 1, core, 0), near_x),
        (half_block(place, 2, core, 1), near_y),
        (pl.ds(pl.multiple_of((2 * place[1] + core) * 2 * ROWS, 2 * ROWS), 2 * ROWS), own),
    )
    for columns, out in jobs:
        for source, owner in ((grads, core), (grads_other, 1 - core)):
            part = products(place, mine, theirs, source, columns)
            out[:, positions_of(owner, width)] = part.astype(out.dtype)


def near(place, mine, theirs, grads, grads_other, read):
    rows, width = read.shape
    return kernel_call(
        near_kernel,
        "near",
        place,
        (mine, theirs, grads, grads_other, read),
        [
            ((ROWS, 2 * width), BF16),
            ((ROWS, 2 * width), BF16),
            ((2 * ROWS, 2 * width), F32),
            ((rows, 2 * width), BF16),
        ],
    )


def join(place, same, cross, whole):
    width = same.shape[1]
    whole[:, positions_of(place[0], width)] = same
    whole[:, positions_of(1 - place[0], width)] = cross


def relay_kernel(place, far_x, far_y, keep_x, keep_y, after, *outs):
    core = place[0]
    for index, (far, keep) in enumerate(((far_x, keep_y), (far_y, keep_x))):
        for which, owner in enumerate((core, 1 - core)):
            outs[2 * index + which][...] = (keep[owner] + far[owner].astype(F32)).astype(BF16)


def relay(place, far_x, far_y, keep_x, keep_y, after):
    shape = keep_x.shape[1:]
    operands = (far_x, far_y, keep_x, keep_y, after)
    return kernel_call(relay_kernel, "relay", place, operands, [(shape, BF16)] * 4)


def finish_kernel(place, own, near_x, near_y, top_same, low_same, top_cross, low_cross, whole, sums, sems):
    core = place[0]
    width = top_same.shape[1]
    copies = []
    for owner, top, low in ((core, top_same, low_same), (1 - core, top_cross, low_cross)):
        columns = positions_of(owner, width)
        for rows, first, second in ((slice(0, ROWS), near_x, top), (slice(ROWS, 2 * ROWS), near_y, low)):
            part = first[:, columns].astype(F32) + second[...].astype(F32)
            sums[rows, columns] = own[rows, columns] + part
            place_rows = pl.ds(rows.start, ROWS)
            copies.append(
                pltpu.make_async_copy(
                    sums.at[place_rows, columns], whole.at[place_rows, columns], sems.at[len(copies)]
                )
            )
            copies[-1].start()
    for copy in copies:
        copy.wait()


def finish(place, *parts):
    shape = parts[0].shape
    vmem_spec = pl.BlockSpec(memory_space=pltpu.VMEM)
    return pl.pallas_call(
        finish_kernel,
        grid_spec=pltpu.PrefetchScalarGridSpec(
            num_scalar_prefetch=1,
            grid=(),
            in_specs=[vmem_spec] * len(parts),
            out_specs=pl.BlockSpec(memory_space=pltpu.HBM),
            scratch_shapes=[pltpu.VMEM(shape, F32), pltpu.SemaphoreType.DMA((4,))],
        ),
        out_shape=jax.ShapeDtypeStruct(shape, F32),
        compiler_params=pltpu.CompilerParams(vmem_limit_bytes=VMEM_BYTES),
        cost_estimate=cost(0.01),
        name="finish",
    )(place, *(in_vmem(part) for part in parts))


def join_kernel(place, same, cross, whole):
    join(place, same[...], cross[...], whole)


def local(square, dp_size, ctx_size, queries, keys, values, decay, beta, inputs, probe):
    tokens = queries.shape[1]
    width = queries.shape[2] // 2
    weighting = math.sqrt(D) / (dp_size * ctx_size * tokens)
    ctx = lax.axis_index("ctx")
    chip = lax.axis_index("dp")
    core = lax.rem(ctx, 2)
    groups = ctx_size // 2
    partner = [(index, index ^ 1) for index in range(ctx_size)]
    mine = inputs[0]
    place = jnp.stack([core, chip])

    def swap(block):
        return lax.ppermute(block, "ctx", partner)

    def send(block, chips, cores):
        pairs = [
            (2 * index + which, 2 * (index ^ chips) + (which ^ cores))
            for index in range(dp_size)
            for which in range(2)
        ]
        return lax.ppermute(block, GROUP, pairs)

    def part(block, index):
        return lax.dynamic_slice_in_dim(block, index * width, width, 1)

    kept, given, own, stack, gates = pack(place, square, queries, keys, values, decay, beta, probe)
    if square:
        stack, mine = lax.optimization_barrier((stack, mine))
        stack = swap(stack)
        theirs = swap(mine)
        x_one = send(kept, 1, 0)
        y_one = send(given, 2, 1)
        x_two = send(given, 1, 1)
        maps = prepare(place, 0, tokens, width, own, (gates,))
        late, *maps = lax.optimization_barrier((kept, *maps))
        y_two = send(late, 2, 0)
        x_one, y_one, *maps = lax.optimization_barrier((x_one, y_one, *maps))
        far_one = send(x_one, 2, 0)
        far_two = send(y_one, 1, 0)
        maps = prepare(place, 1, tokens, width, stack, maps)
        pieces = [kept, stack, x_one, y_one, x_two, y_two, far_one, far_two]
        places = [
            (0, "same"),
            (0, "other"),
            (1, "same"),
            (2, "other"),
            (1, "other"),
            (2, "same"),
            (3, "same"),
            (3, "other"),
        ]
    else:
        stack = swap(stack)
        theirs = swap(mine)
        maps = prepare(place, 0, tokens, width, own, (gates,))
        maps = prepare(place, 1, tokens, width, stack, maps)
        gathered = part(lax.all_gather(probe, GROUP, axis=0, tiled=True), core)
        places = list(range(8))
        rows = D // len(places)
        pieces = [gathered[index * rows : (index + 1) * rows] for index in places]
    def shift(block, by):
        pairs = [
            (index, index + 2 * by)
            for index in range(ctx_size)
            if 0 <= index + 2 * by < ctx_size
        ]
        return lax.ppermute(block, "ctx", pairs)

    entry = None
    if groups > 1:
        entry = jnp.zeros((width // DK, DK, DK), F32)
    read = functools.partial(
        read_values,
        place,
        mine,
        theirs,
        own,
        stack,
        maps,
        places[:6],
        pieces[:6],
    )
    for _ in range(groups - 1):
        entry = shift(read(entry)[3], 1)
    total, read_kept, read_given, unused = read(entry)
    lists = ((0, 2), (1, 3)) if square else ()
    run = functools.partial(
        recur,
        weighting,
        place,
        mine,
        theirs,
        total,
        maps,
        read_given,
        places[6:],
        pieces[6:],
        3,
        lists,
    )
    states = None
    if groups > 1:
        states = (jnp.zeros((width // DK, DK, DK), F32),) * 2
        for _ in range(groups - 1):
            states = (shift(run(states)[1], 1), states[1])
        for _ in range(groups - 1):
            states = (states[0], shift(run(states)[2], -1))
    grads, unused, unused, *shares = run(states)
    build = functools.partial(curvature, place, mine, theirs, grads)
    if not square:
        everything = build(((None, (tuple(range(D // ROWS)),)),), [F32])[0]
        flat = everything.reshape(D, width)
        zero = jnp.zeros_like(flat)
        both = jnp.where(
            core == 0, jnp.concatenate([flat, zero], 1), jnp.concatenate([zero, flat], 1)
        )
        read_swapped = swap(read_given)
        mixed = kernel_call(
            join_kernel, "join", place, (read_kept, read_swapped), [((tokens, 2 * width), BF16)]
        )[0]
        return mixed[None], lax.psum_scatter(both, GROUP, scatter_dimension=0, tiled=True)

    far_x = send(shares[0], 1, 0)
    far_y = send(shares[1], 2, 0)
    grads_other = swap(grads)
    keep_x, keep_y = keep(place, mine, theirs, grads)
    near_x, near_y, rest, mixed = near(place, mine, theirs, grads, grads_other, read_kept)
    after = near_x
    near_x = send(near_x, 1, 0)
    near_y = send(near_y, 2, 0)
    top_same, top_cross, low_same, low_cross = relay(place, far_x, far_y, keep_x, keep_y, after)
    top_same = send(top_same, 2, 0)
    low_same = send(low_same, 1, 0)
    near_x, low_cross = lax.optimization_barrier((near_x, low_cross))
    top_cross = send(top_cross, 2, 1)
    low_cross = send(low_cross, 1, 1)
    result = finish(place, rest, near_x, near_y, top_same, low_same, top_cross, low_cross)
    return mixed[None], result


def solution(mesh):
    dp_size, ctx_size = mesh.shape["dp"], mesh.shape["ctx"]
    square = dp_size == 4 and ctx_size == 2
    return jax.shard_map(
        functools.partial(local, square, dp_size, ctx_size),
        mesh=mesh,
        in_specs=(
            P("dp", "ctx", "head"),
            P("dp", "ctx", "head"),
            P("dp", "ctx", "head"),
            P("dp", "head", "ctx"),
            P("dp", "head", "ctx"),
            P("dp", "ctx", None),
            P(("dp", "ctx"), "head"),
        ),
        out_specs=(P("dp", "ctx", "head"), P(("dp", "ctx"), "head")),
        check_vma=False,
    )
```

```python
import functools
import math

import jax
import jax.numpy as jnp
from jax import lax
from jax.experimental import pallas as pl
from jax.experimental.pallas import tpu as pltpu
from jax.sharding import PartitionSpec as P

D = 4096
DK = 128
SPAN = 128
EPSILON = 1e-06
GROUP = ("dp", "ctx")
BF16 = jnp.bfloat16
F32 = jnp.float32
VMEM_BYTES = 24 * 1024 * 1024


def cost(us):
    return pl.CostEstimate(flops=int(us * 1.1e9), bytes_accessed=int(us * 3.0e6), transcendentals=0)


def in_hbm(block):
    return pltpu.with_memory_space_constraint(block, pltpu.HBM)


def in_vmem(block):
    return pltpu.with_memory_space_constraint(block, pltpu.VMEM)


def kernel_call(kernel, name, place, operands, outs, scratch=(), aliases=None, far=()):
    vmem_spec = pl.BlockSpec(memory_space=pltpu.VMEM)
    return pl.pallas_call(
        kernel,
        grid_spec=pltpu.PrefetchScalarGridSpec(
            num_scalar_prefetch=1,
            grid=(),
            in_specs=[pl.BlockSpec(memory_space=pltpu.HBM)] * len(far) + [vmem_spec] * len(operands),
            out_specs=[vmem_spec] * len(outs),
            scratch_shapes=list(scratch),
        ),
        out_shape=[jax.ShapeDtypeStruct(shape, kind) for shape, kind in outs],
        input_output_aliases=aliases or {},
        compiler_params=pltpu.CompilerParams(vmem_limit_bytes=VMEM_BYTES),
        cost_estimate=cost(0.01),
        name=name,
    )(place, *(in_hbm(block) for block in far), *(in_vmem(block) for block in operands))


def dot(left, right):
    return jnp.dot(left, right, preferred_element_type=F32)


def dot_nt(left, right):
    return lax.dot_general(left, right, (((1,), (1,)), ((), ())), preferred_element_type=F32)


def halves(block):
    high = block.astype(BF16)
    return high, (block - high.astype(F32)).astype(BF16)


def fine_dot(left, right):
    left_high, left_low = halves(left)
    right_high, right_low = halves(right)
    wide = jnp.concatenate([right_high, right_low], 1)
    both = dot(jnp.concatenate([left_high, left_low], 1), jnp.concatenate([wide, wide], 0))
    width = right.shape[1]
    return both[:, :width] + both[:, width:]


def unit(block):
    block = block.astype(F32)
    return (block * lax.rsqrt(jnp.sum(block * block, -1, keepdims=True) + EPSILON)).astype(BF16)


GATE_ROWS = 32


def terms_of(block):
    terms = []
    for _ in range(3):
        term = block.astype(BF16)
        terms.append(term.astype(F32))
        block = block - terms[-1]
    return terms


def pack_kernel(place, queries, keys, values, decay, beta, probe, kept, given, own, stack, gates, sems):
    core = place[0]
    tokens, width = own.shape[1:]
    same = pl.ds(pl.multiple_of(core * width, width), width)
    cross = pl.ds(pl.multiple_of((1 - core) * width, width), width)
    slots = [pl.ds(i * tokens, tokens) for i in range(4)]
    moves = [(decay.at[0], gates.at[0]), (beta.at[0], gates.at[1])]
    moves += [(probe.at[:, same], kept), (probe.at[:, cross], given)]
    moves += [
        (block.at[0, :, cross], stack.at[slots[i], :]) for i, block in enumerate((queries, keys, values))
    ]
    if stack.shape[0] > 4 * tokens:
        moves.append((probe.at[:, cross], stack.at[slots[3], :]))
    moves += [(block.at[0, :, same], own.at[i]) for i, block in enumerate((queries, keys, values))]
    copies = [
        pltpu.make_async_copy(source, target, sems.at[i]) for i, (source, target) in enumerate(moves)
    ]
    for copy in copies:
        copy.start()
    copies[0].wait()
    copies[1].wait()
    heads = gates.shape[1] // 2
    rows = []
    for kind in range(2):
        block = jnp.where(core == 0, gates[kind, heads:], gates[kind, :heads])
        for term in terms_of(block):
            rows += [term[:, begin : begin + width] for begin in range(0, tokens, width)]
    used = sum(row.shape[0] for row in rows)
    rows.append(jnp.zeros((GATE_ROWS - used, width), F32))
    stack[stack.shape[0] - GATE_ROWS :, :] = jnp.concatenate(rows, 0).astype(BF16)
    for copy in copies[2:]:
        copy.wait()


def received_gates(stack, tokens, heads):
    width = stack.shape[1]
    block = stack[stack.shape[0] - GATE_ROWS :, :].astype(F32)
    cuts = tokens // width
    out = []
    for kind in range(2):
        terms = []
        for term in range(3):
            begin = (kind * 3 + term) * cuts * heads
            terms.append(
                jnp.concatenate(
                    [block[begin + cut * heads : begin + (cut + 1) * heads] for cut in range(cuts)], 1
                )
            )
        out.append(terms[0] + terms[1] + terms[2])
    return out


def pack(place, with_probe, queries, keys, values, decay, beta, probe):
    tokens = queries.shape[1]
    width = queries.shape[2] // 2
    hbm_spec = pl.BlockSpec(memory_space=pltpu.HBM)
    vmem_spec = pl.BlockSpec(memory_space=pltpu.VMEM)
    half = jax.ShapeDtypeStruct((probe.shape[0], width), BF16)
    return pl.pallas_call(
        pack_kernel,
        grid_spec=pltpu.PrefetchScalarGridSpec(
            num_scalar_prefetch=1,
            grid=(),
            in_specs=[hbm_spec] * 6,
            out_specs=[vmem_spec] * 5,
            scratch_shapes=[pltpu.SemaphoreType.DMA((11,))],
        ),
        out_shape=[
            half,
            half,
            jax.ShapeDtypeStruct((3, tokens, width), BF16),
            jax.ShapeDtypeStruct(((4 if with_probe else 3) * tokens + GATE_ROWS, width), BF16),
            jax.ShapeDtypeStruct((2,) + decay.shape[1:], F32),
        ],
        compiler_params=pltpu.CompilerParams(vmem_limit_bytes=VMEM_BYTES),
        cost_estimate=cost(0.01),
        name="pack",
    )(place, *(in_hbm(block) for block in (queries, keys, values, decay, beta, probe)))


def prepare_kernel(side, tokens, place, stack, *refs):
    forth, back, back_low = refs[-3:]
    core = place[0]
    owner = core if side == 0 else 1 - core
    if side == 0:
        queries, keys = stack[0], stack[1]
    else:
        queries, keys = stack[:tokens], stack[tokens : 2 * tokens]
    width = queries.shape[1]
    spans, heads = tokens // SPAN, width // DK
    rows = lax.broadcasted_iota(jnp.int32, (SPAN, SPAN), 0)
    cols = lax.broadcasted_iota(jnp.int32, (SPAN, SPAN), 1)
    inclusive = rows >= cols
    strict = rows > cols
    diagonal = rows == cols
    items = [(span, head) for span in range(spans) for head in range(heads)]


    def cut(block, item):
        span, head = item
        return block[span * SPAN : (span + 1) * SPAN, head * DK : (head + 1) * DK]

    def cut_row(block, item):
        span, head = item
        return block[head : head + 1, span * SPAN : (span + 1) * SPAN]

    def column_of(row):
        return jnp.sum(jnp.where(diagonal, row, 0.0), 1, keepdims=True)

    def row_of(column):
        return jnp.sum(jnp.where(diagonal, column, 0.0), 0, keepdims=True)

    def lower_left(size):
        return (
            (rows // (2 * size) == cols // (2 * size))
            & ((rows // size) % 2 == 1)
            & ((cols // size) % 2 == 0)
        )

    if side == 0:
        gates = refs[0]
        decays, strengths = [
            jnp.where(core == 0, gates[kind, :heads], gates[kind, heads:]) for kind in range(2)
        ]
    else:
        decays, strengths = received_gates(stack, tokens, heads)
    decay_log = jnp.log(decays)
    identity = jnp.where(diagonal, 1.0, 0.0)

    def build(items):
        q = [unit(cut(queries, item)) for item in items]
        k = [unit(cut(keys, item)) for item in items]
        growth_log = [
            jnp.sum(jnp.where(inclusive, cut_row(decay_log, item), 0.0), 1, keepdims=True)
            for item in items
        ]
        strength_row = [cut_row(strengths, item) for item in items]
        inner = [dot_nt(jnp.concatenate([kk, qq], 0), kk) for kk, qq in zip(k, q)]
        ratios = [
            jnp.where(inclusive, jnp.exp(jnp.where(inclusive, log - row_of(log), 0.0)), 0.0)
            for log in growth_log
        ]
        coupling = [
            jnp.where(strict, column_of(row) * ratio * both[:SPAN], 0.0)
            for row, ratio, both in zip(strength_row, ratios, inner)
        ]
        mixing = [ratio * both[SPAN:] for ratio, both in zip(ratios, inner)]
        corner = lower_left(1)
        inverse = [identity - jnp.where(corner, block, 0.0) for block in coupling]
        size = 2
        while size < SPAN:
            corner = lower_left(size)
            narrow = [block.astype(BF16) for block in inverse]
            part = [
                dot(x, jnp.where(corner, a, 0.0).astype(BF16)) for x, a in zip(narrow, coupling)
            ]
            step_back = [dot(y.astype(BF16), x) for y, x in zip(part, narrow)]
            inverse = [x - z for x, z in zip(inverse, step_back)]
            size *= 2
        residual = [identity - x - fine_dot(a, x) for a, x in zip(coupling, inverse)]
        inverse = [x + dot(x.astype(BF16), e.astype(BF16)) for x, e in zip(inverse, residual)]
        scaled = [x * row for x, row in zip(inverse, strength_row)]
        growth = [jnp.exp(log) for log in growth_log]
        grown_keys = [g * kk.astype(F32) for g, kk in zip(growth, k)]
        grown_queries = [g * qq.astype(F32) for g, qq in zip(growth, q)]
        tails = [
            (jnp.exp(log[SPAN - 1 :] - log) * kk.astype(F32)).T for log, kk in zip(growth_log, k)
        ]
        upper = [
            fine_dot(jnp.concatenate([tail, mix], 0), b)
            for tail, mix, b in zip(tails, mixing, scaled)
        ]
        removed = [fine_dot(up, gk) for up, gk in zip(upper, grown_keys)]
        for item, g, up, rem, gq in zip(items, growth, upper, removed, grown_queries):
            span, head = item
            kept = jnp.where(diagonal, g[SPAN - 1 :], 0.0)
            whole = jnp.concatenate([jnp.concatenate([kept, gq], 0) - rem, up], 1)
            high, low = halves(whole.T)
            forth[owner, span, head] = whole.astype(BF16)
            back[owner, span, head] = high
            back_low[owner, span, head] = low

    for start in range(0, len(items), BATCH):
        build(items[start : start + BATCH])


BATCH = 8


def prepare(place, side, tokens, width, stack, others):
    heads = width // DK
    shape = (2, tokens // SPAN, heads, 2 * DK, 2 * DK)
    return kernel_call(
        functools.partial(prepare_kernel, side, tokens),
        "prepare",
        place,
        (stack,) + tuple(others),
        [(shape, BF16)] * 3,
        aliases={2 + index: index for index in range(3)} if side else {},
    )


def owned(place, blocks):
    mine, theirs = blocks
    first = place[0] == 0
    return jnp.where(first, mine, theirs), jnp.where(first, theirs, mine)


def row_block(place, block):
    if isinstance(block, int):
        return block
    chips, core = block
    if core == "same":
        core = place[0]
    elif core == "other":
        core = 1 - place[0]
    return 2 * lax.bitwise_xor(place[1], chips) + core


def columns_of(place, block, width):
    return pl.ds(pl.multiple_of(row_block(place, block) * width, width), width)


def positions_of(owner, tokens):
    return pl.ds(pl.multiple_of(owner * tokens, tokens), tokens)


def load_piece(ref, rows):
    return ref[:rows] if ref.shape[0] < 3 * rows else ref[3 * rows : 4 * rows]


def read_kernel(with_state, blocks, place, mine, theirs, own, stack, back, low, *refs):
    count = len(blocks)
    pieces, refs = refs[:count], refs[count:]
    if with_state:
        (first, *refs) = refs
    (total, kept, given, last, read) = refs
    tokens, width = own.shape[1:]
    spans, heads = back.shape[1:3]
    core = place[0]
    values = owned(place, (own[2], stack[2 * tokens : 3 * tokens]))
    products = product_steps(place, blocks, mine, theirs, pieces, total, None)
    zero = jnp.zeros((DK, DK), F32)
    states = [first[head] if with_state else zero for head in range(heads)]
    for half in range(2):
        for span in range(spans):
            for head in range(heads):
                positions = slice(span * SPAN, (span + 1) * SPAN)
                columns = slice(head * DK, (head + 1) * DK)
                block = values[half][positions, columns].T
                x_high, x_low = halves(states[head])
                left = jnp.concatenate([x_high, block], 1)
                rest = jnp.concatenate([x_low, jnp.zeros_like(block)], 1)
                both = dot(jnp.concatenate([left, rest], 0), back[half, span, head])
                result = both[:DK] + both[DK:] + dot(left, low[half, span, head])
                states[head] = result[:, :DK]
                read[half, positions, columns] = result[:, DK:].T.astype(BF16)
            next(products, None)
    for head in range(heads):
        last[head] = states[head]
    for _ in products:
        pass
    kept[...] = read[core]
    given[...] = read[1 - core]


def paired(blocks):
    return not isinstance(blocks[0], int) and blocks[0][0] == blocks[1][0]


def add_products(place, blocks, mine, theirs, pieces, result, total):
    for _ in product_steps(place, blocks, mine, theirs, pieces, result, total):
        pass


def product_steps(place, blocks, mine, theirs, pieces, result, total):
    tokens = mine.shape[0]
    rows = mine.shape[1] // 8
    core = place[0]
    probe = [load_piece(piece, rows) for piece in pieces]
    for source, owner in ((mine, core), (theirs, 1 - core)):
        positions = positions_of(owner, tokens)
        begin = 0
        part = None if total is None else total[positions, :]
        if paired(blocks):
            chip = lax.bitwise_xor(place[1], blocks[0][0])
            columns = pl.ds(pl.multiple_of(chip * 2 * rows, 2 * rows), 2 * rows)
            product = dot(source[:, columns], jnp.concatenate(owned(place, probe[:2]), 0))
            part = product if part is None else part + product
            begin = 2
            yield
        for block, piece in zip(blocks[begin:], probe[begin:]):
            product = dot(source[:, columns_of(place, block, rows)], piece)
            part = product if part is None else part + product
            yield
        result[positions, :] = part.astype(result.dtype)


def read_values(place, mine, theirs, own, stack, maps, blocks, pieces, entry):
    tokens, width = own.shape[1:]
    heads = width // DK
    extra = () if entry is None else (entry,)
    return kernel_call(
        functools.partial(read_kernel, entry is not None, tuple(blocks)),
        "read_values",
        place,
        (mine, theirs, own, stack, maps[1], maps[2], *pieces, *extra),
        [
            ((2 * tokens, width), F32),
            ((tokens, width), BF16),
            ((tokens, width), BF16),
            ((heads, DK, DK), F32),
        ],
        scratch=[pltpu.VMEM((2, tokens, width), BF16)],
    )


def recur_kernel(weighting, with_state, blocks, chips, lists, place, mine, theirs, total, forth, back, read, *refs):
    count = len(blocks)
    pieces, refs = refs[:count], refs[count:]
    if with_state:
        (first, final, *refs) = refs
    (grads, last, start, *refs) = refs
    width = total.shape[1]
    shares, (sums, up) = refs[: len(lists)], refs[len(lists) :]
    tokens = mine.shape[0]
    spans, heads = forth.shape[1:3]
    add_products(place, blocks, mine, theirs, pieces, sums, total)
    zero = jnp.zeros((DK, DK), F32)
    states = [first[head] if with_state else zero for head in range(heads)]
    steps = [(half, span) for half in range(2) for span in range(spans)]
    for half, span in steps:
        begin = half * tokens + span * SPAN
        for head in range(heads):
            block = sums[begin : begin + SPAN, head * DK : (head + 1) * DK].T.astype(BF16)
            left = jnp.concatenate([states[head].astype(BF16), block], 1)
            result = dot(left, back[half, span, head])
            states[head] = result[:, :DK]
            up[half, span, head] = (weighting * result[:, DK:]).astype(BF16)
    for head in range(heads):
        last[head] = states[head]
    states = [final[head] if with_state else zero for head in range(heads)]
    for half, span in reversed(steps):
        begin = half * tokens + span * SPAN
        for head in range(heads):
            left = jnp.concatenate([states[head].astype(BF16), up[half, span, head]], 1)
            result = dot(left, forth[half, span, head])
            states[head] = result[:, :DK]
            row = begin // width * width + head * DK
            grads[row : row + DK, begin % width : begin % width + SPAN] = result[:, DK:].astype(BF16)
    grads[2 * tokens :, :] = read[...]
    for head in range(heads):
        start[head] = states[head]
    if lists:
        put_products(place, chips, lists, mine, theirs, grads, shares)


def grads_of(grads, owner, tokens):
    width = grads.shape[1]
    block = grads[positions_of(owner, tokens), :]
    return jnp.concatenate([block[i : i + width] for i in range(0, tokens, width)], 1)


def put_products(place, chips, lists, mine, theirs, grads, outs):
    tokens, width = mine.shape
    if chips is None:
        columns = pl.ds(0, width)
    else:
        columns = pl.ds(pl.multiple_of(lax.bitwise_xor(place[1], chips) * 4 * ROWS, 4 * ROWS), 4 * ROWS)
    core = place[0]
    part = dot(grads_of(grads, core, tokens), mine[:, columns])
    part += dot(grads_of(grads, 1 - core, tokens), theirs[:, columns])
    part = part.T
    for out, indices in zip(outs, lists):
        for slot, index in enumerate(indices):
            out[slot] = part[index * ROWS : (index + 1) * ROWS].astype(out.dtype)


def recur(weighting, place, mine, theirs, total, maps, read, blocks, pieces, chips, lists, states):
    tokens = mine.shape[0]
    width = total.shape[1]
    spans, heads = maps[0].shape[1:3]
    extra = () if states is None else states
    return kernel_call(
        functools.partial(
            recur_kernel, weighting, states is not None, tuple(blocks), chips, lists
        ),
        "recur",
        place,
        (mine, theirs, total, maps[0], maps[1], read, *pieces, *extra),
        [((3 * tokens, width), BF16), ((heads, DK, DK), F32), ((heads, DK, DK), F32)]
        + [((len(part), ROWS, width), BF16) for part in lists],
        scratch=[
            pltpu.VMEM((2 * tokens, width), F32),
            pltpu.VMEM((2, spans, heads, DK, SPAN), BF16),
        ],
    )


ROWS = 256


def curvature_kernel(jobs, place, mine, theirs, grads, *outs):
    begin = 0
    for chips, lists in jobs:
        put_products(place, chips, lists, mine, theirs, grads, outs[begin : begin + len(lists)])
        begin += len(lists)


def curvature(place, mine, theirs, grads, jobs, types):
    width = grads.shape[1]
    lengths = [len(part) for chips, lists in jobs for part in lists]
    return kernel_call(
        functools.partial(curvature_kernel, jobs),
        "curvature",
        place,
        (mine, theirs, grads),
        [((length, ROWS, width), kind) for length, kind in zip(lengths, types)],
    )


def keep_kernel(place, mine, theirs, grads, keep_x, keep_y):
    for chips, half, out in ((1, 1, keep_x), (2, 0, keep_y)):
        for block in range(2):
            columns = half_block(place, chips, block, half)
            out[block] = products(place, mine, theirs, grads, columns)


def half_block(place, chips, block, half):
    index = 2 * (2 * lax.bitwise_xor(place[1], chips) + block) + half
    return pl.ds(pl.multiple_of(index * ROWS, ROWS), ROWS)


def products(place, mine, theirs, grads, columns):
    tokens = mine.shape[0]
    core = place[0]
    part = dot(grads_of(grads, core, tokens), mine[:, columns])
    part += dot(grads_of(grads, 1 - core, tokens), theirs[:, columns])
    return part.T


def keep(place, mine, theirs, grads):
    shape = (2, ROWS, grads.shape[1])
    return kernel_call(keep_kernel, "keep", place, (mine, theirs, grads), [(shape, F32)] * 2)


def near_kernel(place, mine, theirs, grads, grads_other, read, near_x, near_y, own, mixed):
    core = place[0]
    tokens, width = read.shape
    join(place, read[...], grads_other[2 * tokens :, :], mixed)
    jobs = (
        (half_block(place, 1, core, 0), near_x),
        (half_block(place, 2, core, 1), near_y),
        (pl.ds(pl.multiple_of((2 * place[1] + core) * 2 * ROWS, 2 * ROWS), 2 * ROWS), own),
    )
    for columns, out in jobs:
        for source, owner in ((grads, core), (grads_other, 1 - core)):
            part = products(place, mine, theirs, source, columns)
            out[:, positions_of(owner, width)] = part.astype(out.dtype)


def near(place, mine, theirs, grads, grads_other, read):
    rows, width = read.shape
    return kernel_call(
        near_kernel,
        "near",
        place,
        (mine, theirs, grads, grads_other, read),
        [
            ((ROWS, 2 * width), BF16),
            ((ROWS, 2 * width), BF16),
            ((2 * ROWS, 2 * width), F32),
            ((rows, 2 * width), BF16),
        ],
    )


def join(place, same, cross, whole):
    width = same.shape[1]
    whole[:, positions_of(place[0], width)] = same
    whole[:, positions_of(1 - place[0], width)] = cross


def relay_kernel(place, far_x, far_y, keep_x, keep_y, after, *outs):
    core = place[0]
    for index, (far, keep) in enumerate(((far_x, keep_y), (far_y, keep_x))):
        for which, owner in enumerate((core, 1 - core)):
            outs[2 * index + which][...] = (keep[owner] + far[owner].astype(F32)).astype(BF16)


def relay(place, far_x, far_y, keep_x, keep_y, after):
    shape = keep_x.shape[1:]
    operands = (far_x, far_y, keep_x, keep_y, after)
    return kernel_call(relay_kernel, "relay", place, operands, [(shape, BF16)] * 4)


def finish_kernel(place, own, near_x, near_y, top_same, low_same, top_cross, low_cross, whole, sums, sems):
    core = place[0]
    width = top_same.shape[1]
    copies = []
    for owner, top, low in ((core, top_same, low_same), (1 - core, top_cross, low_cross)):
        columns = positions_of(owner, width)
        for rows, first, second in ((slice(0, ROWS), near_x, top), (slice(ROWS, 2 * ROWS), near_y, low)):
            part = first[:, columns].astype(F32) + second[...].astype(F32)
            sums[rows, columns] = own[rows, columns] + part
            place_rows = pl.ds(rows.start, ROWS)
            copies.append(
                pltpu.make_async_copy(
                    sums.at[place_rows, columns], whole.at[place_rows, columns], sems.at[len(copies)]
                )
            )
            copies[-1].start()
    for copy in copies:
        copy.wait()


def finish(place, *parts):
    shape = parts[0].shape
    vmem_spec = pl.BlockSpec(memory_space=pltpu.VMEM)
    return pl.pallas_call(
        finish_kernel,
        grid_spec=pltpu.PrefetchScalarGridSpec(
            num_scalar_prefetch=1,
            grid=(),
            in_specs=[vmem_spec] * len(parts),
            out_specs=pl.BlockSpec(memory_space=pltpu.HBM),
            scratch_shapes=[pltpu.VMEM(shape, F32), pltpu.SemaphoreType.DMA((4,))],
        ),
        out_shape=jax.ShapeDtypeStruct(shape, F32),
        compiler_params=pltpu.CompilerParams(vmem_limit_bytes=VMEM_BYTES),
        cost_estimate=cost(0.01),
        name="finish",
    )(place, *(in_vmem(part) for part in parts))


def join_kernel(place, same, cross, whole):
    join(place, same[...], cross[...], whole)


def local(square, dp_size, ctx_size, queries, keys, values, decay, beta, inputs, probe):
    tokens = queries.shape[1]
    width = queries.shape[2] // 2
    weighting = math.sqrt(D) / (dp_size * ctx_size * tokens)
    ctx = lax.axis_index("ctx")
    chip = lax.axis_index("dp")
    core = lax.rem(ctx, 2)
    groups = ctx_size // 2
    partner = [(index, index ^ 1) for index in range(ctx_size)]
    mine = inputs[0]
    place = jnp.stack([core, chip])

    def swap(block):
        return lax.ppermute(block, "ctx", partner)

    def send(block, chips, cores):
        pairs = [
            (2 * index + which, 2 * (index ^ chips) + (which ^ cores))
            for index in range(dp_size)
            for which in range(2)
        ]
        return lax.ppermute(block, GROUP, pairs)

    def part(block, index):
        return lax.dynamic_slice_in_dim(block, index * width, width, 1)

    kept, given, own, stack, gates = pack(place, square, queries, keys, values, decay, beta, probe)
    if square:
        stack, mine = lax.optimization_barrier((stack, mine))
        stack = swap(stack)
        theirs = swap(mine)
        x_one = send(kept, 1, 0)
        y_one = send(given, 2, 1)
        y_two = send(kept, 2, 0)
        maps = prepare(place, 0, tokens, width, own, (gates,))
        late, *maps = lax.optimization_barrier((given, *maps))
        x_two = send(late, 1, 1)
        x_one, y_one, *maps = lax.optimization_barrier((x_one, y_one, *maps))
        far_one = send(x_one, 2, 0)
        far_two = send(y_one, 1, 0)
        maps = prepare(place, 1, tokens, width, stack, maps)
        pieces = [kept, stack, x_one, y_one, x_two, y_two, far_one, far_two]
        places = [
            (0, "same"),
            (0, "other"),
            (1, "same"),
            (2, "other"),
            (1, "other"),
            (2, "same"),
            (3, "same"),
            (3, "other"),
        ]
    else:
        stack = swap(stack)
        theirs = swap(mine)
        maps = prepare(place, 0, tokens, width, own, (gates,))
        maps = prepare(place, 1, tokens, width, stack, maps)
        gathered = part(lax.all_gather(probe, GROUP, axis=0, tiled=True), core)
        places = list(range(8))
        rows = D // len(places)
        pieces = [gathered[index * rows : (index + 1) * rows] for index in places]
    def shift(block, by):
        pairs = [
            (index, index + 2 * by)
            for index in range(ctx_size)
            if 0 <= index + 2 * by < ctx_size
        ]
        return lax.ppermute(block, "ctx", pairs)

    entry = None
    if groups > 1:
        entry = jnp.zeros((width // DK, DK, DK), F32)
    read = functools.partial(
        read_values,
        place,
        mine,
        theirs,
        own,
        stack,
        maps,
        places[:6],
        pieces[:6],
    )
    for _ in range(groups - 1):
        entry = shift(read(entry)[3], 1)
    total, read_kept, read_given, unused = read(entry)
    lists = ((0, 2), (1, 3)) if square else ()
    run = functools.partial(
        recur,
        weighting,
        place,
        mine,
        theirs,
        total,
        maps,
        read_given,
        places[6:],
        pieces[6:],
        3,
        lists,
    )
    states = None
    if groups > 1:
        states = (jnp.zeros((width // DK, DK, DK), F32),) * 2
        for _ in range(groups - 1):
            states = (shift(run(states)[1], 1), states[1])
        for _ in range(groups - 1):
            states = (states[0], shift(run(states)[2], -1))
    grads, unused, unused, *shares = run(states)
    build = functools.partial(curvature, place, mine, theirs, grads)
    if not square:
        everything = build(((None, (tuple(range(D // ROWS)),)),), [F32])[0]
        flat = everything.reshape(D, width)
        zero = jnp.zeros_like(flat)
        both = jnp.where(
            core == 0, jnp.concatenate([flat, zero], 1), jnp.concatenate([zero, flat], 1)
        )
        read_swapped = swap(read_given)
        mixed = kernel_call(
            join_kernel, "join", place, (read_kept, read_swapped), [((tokens, 2 * width), BF16)]
        )[0]
        return mixed[None], lax.psum_scatter(both, GROUP, scatter_dimension=0, tiled=True)

    far_x = send(shares[0], 1, 0)
    far_y = send(shares[1], 2, 0)
    grads_other = swap(grads)
    keep_x, keep_y = keep(place, mine, theirs, grads)
    near_x, near_y, rest, mixed = near(place, mine, theirs, grads, grads_other, read_kept)
    after = near_x
    near_x = send(near_x, 1, 0)
    near_y = send(near_y, 2, 0)
    top_same, top_cross, low_same, low_cross = relay(place, far_x, far_y, keep_x, keep_y, after)
    top_same = send(top_same, 2, 0)
    low_same = send(low_same, 1, 0)
    near_x, low_cross = lax.optimization_barrier((near_x, low_cross))
    top_cross = send(top_cross, 2, 1)
    low_cross = send(low_cross, 1, 1)
    result = finish(place, rest, near_x, near_y, top_same, low_same, top_cross, low_cross)
    return mixed[None], result


def solution(mesh):
    dp_size, ctx_size = mesh.shape["dp"], mesh.shape["ctx"]
    square = dp_size == 4 and ctx_size == 2
    return jax.shard_map(
        functools.partial(local, square, dp_size, ctx_size),
        mesh=mesh,
        in_specs=(
            P("dp", "ctx", "head"),
            P("dp", "ctx", "head"),
            P("dp", "ctx", "head"),
            P("dp", "head", "ctx"),
            P("dp", "head", "ctx"),
            P("dp", "ctx", None),
            P(("dp", "ctx"), "head"),
        ),
        out_specs=(P("dp", "ctx", "head"), P(("dp", "ctx"), "head")),
        check_vma=False,
    )
```

```python
import functools
import math

import jax
import jax.numpy as jnp
from jax import lax
from jax.experimental import pallas as pl
from jax.experimental.pallas import tpu as pltpu
from jax.sharding import PartitionSpec as P

D = 4096
DK = 128
SPAN = 128
EPSILON = 1e-06
GROUP = ("dp", "ctx")
BF16 = jnp.bfloat16
F32 = jnp.float32
VMEM_BYTES = 24 * 1024 * 1024


def cost(us):
    return pl.CostEstimate(flops=int(us * 1.1e9), bytes_accessed=int(us * 3.0e6), transcendentals=0)


def in_hbm(block):
    return pltpu.with_memory_space_constraint(block, pltpu.HBM)


def in_vmem(block):
    return pltpu.with_memory_space_constraint(block, pltpu.VMEM)


def kernel_call(kernel, name, place, operands, outs, scratch=(), aliases=None, far=()):
    vmem_spec = pl.BlockSpec(memory_space=pltpu.VMEM)
    return pl.pallas_call(
        kernel,
        grid_spec=pltpu.PrefetchScalarGridSpec(
            num_scalar_prefetch=1,
            grid=(),
            in_specs=[pl.BlockSpec(memory_space=pltpu.HBM)] * len(far) + [vmem_spec] * len(operands),
            out_specs=[vmem_spec] * len(outs),
            scratch_shapes=list(scratch),
        ),
        out_shape=[jax.ShapeDtypeStruct(shape, kind) for shape, kind in outs],
        input_output_aliases=aliases or {},
        compiler_params=pltpu.CompilerParams(vmem_limit_bytes=VMEM_BYTES),
        cost_estimate=cost(0.01),
        name=name,
    )(place, *(in_hbm(block) for block in far), *(in_vmem(block) for block in operands))


def dot(left, right):
    return jnp.dot(left, right, preferred_element_type=F32)


def dot_nt(left, right):
    return lax.dot_general(left, right, (((1,), (1,)), ((), ())), preferred_element_type=F32)


def halves(block):
    high = block.astype(BF16)
    return high, (block - high.astype(F32)).astype(BF16)


def fine_dot(left, right):
    left_high, left_low = halves(left)
    right_high, right_low = halves(right)
    wide = jnp.concatenate([right_high, right_low], 1)
    both = dot(jnp.concatenate([left_high, left_low], 1), jnp.concatenate([wide, wide], 0))
    width = right.shape[1]
    return both[:, :width] + both[:, width:]


def unit(block):
    block = block.astype(F32)
    return (block * lax.rsqrt(jnp.sum(block * block, -1, keepdims=True) + EPSILON)).astype(BF16)


GATE_ROWS = 32


def terms_of(block):
    terms = []
    for _ in range(3):
        term = block.astype(BF16)
        terms.append(term.astype(F32))
        block = block - terms[-1]
    return terms


def pack_kernel(place, queries, keys, values, decay, beta, probe, kept, given, own, stack, gates, sems):
    core = place[0]
    tokens, width = own.shape[1:]
    same = pl.ds(pl.multiple_of(core * width, width), width)
    cross = pl.ds(pl.multiple_of((1 - core) * width, width), width)
    slots = [pl.ds(i * tokens, tokens) for i in range(4)]
    moves = [(decay.at[0], gates.at[0]), (beta.at[0], gates.at[1])]
    moves += [(probe.at[:, same], kept), (probe.at[:, cross], given)]
    moves += [
        (block.at[0, :, cross], stack.at[slots[i], :]) for i, block in enumerate((queries, keys, values))
    ]
    if stack.shape[0] > 4 * tokens:
        moves.append((probe.at[:, cross], stack.at[slots[3], :]))
    moves += [(block.at[0, :, same], own.at[i]) for i, block in enumerate((queries, keys, values))]
    copies = [
        pltpu.make_async_copy(source, target, sems.at[i]) for i, (source, target) in enumerate(moves)
    ]
    for copy in copies:
        copy.start()
    copies[0].wait()
    copies[1].wait()
    heads = gates.shape[1] // 2
    rows = []
    for kind in range(2):
        block = jnp.where(core == 0, gates[kind, heads:], gates[kind, :heads])
        for term in terms_of(block):
            rows += [term[:, begin : begin + width] for begin in range(0, tokens, width)]
    used = sum(row.shape[0] for row in rows)
    rows.append(jnp.zeros((GATE_ROWS - used, width), F32))
    stack[stack.shape[0] - GATE_ROWS :, :] = jnp.concatenate(rows, 0).astype(BF16)
    for copy in copies[2:]:
        copy.wait()


def received_gates(stack, tokens, heads):
    width = stack.shape[1]
    block = stack[stack.shape[0] - GATE_ROWS :, :].astype(F32)
    cuts = tokens // width
    out = []
    for kind in range(2):
        terms = []
        for term in range(3):
            begin = (kind * 3 + term) * cuts * heads
            terms.append(
                jnp.concatenate(
                    [block[begin + cut * heads : begin + (cut + 1) * heads] for cut in range(cuts)], 1
                )
            )
        out.append(terms[0] + terms[1] + terms[2])
    return out


def pack(place, with_probe, queries, keys, values, decay, beta, probe):
    tokens = queries.shape[1]
    width = queries.shape[2] // 2
    hbm_spec = pl.BlockSpec(memory_space=pltpu.HBM)
    vmem_spec = pl.BlockSpec(memory_space=pltpu.VMEM)
    half = jax.ShapeDtypeStruct((probe.shape[0], width), BF16)
    return pl.pallas_call(
        pack_kernel,
        grid_spec=pltpu.PrefetchScalarGridSpec(
            num_scalar_prefetch=1,
            grid=(),
            in_specs=[hbm_spec] * 6,
            out_specs=[vmem_spec] * 5,
            scratch_shapes=[pltpu.SemaphoreType.DMA((11,))],
        ),
        out_shape=[
            half,
            half,
            jax.ShapeDtypeStruct((3, tokens, width), BF16),
            jax.ShapeDtypeStruct(((4 if with_probe else 3) * tokens + GATE_ROWS, width), BF16),
            jax.ShapeDtypeStruct((2,) + decay.shape[1:], F32),
        ],
        compiler_params=pltpu.CompilerParams(vmem_limit_bytes=VMEM_BYTES),
        cost_estimate=cost(0.01),
        name="pack",
    )(place, *(in_hbm(block) for block in (queries, keys, values, decay, beta, probe)))


def prepare_kernel(side, tokens, place, stack, *refs):
    forth, back, back_low = refs[-3:]
    core = place[0]
    owner = core if side == 0 else 1 - core
    if side == 0:
        queries, keys = stack[0], stack[1]
    else:
        queries, keys = stack[:tokens], stack[tokens : 2 * tokens]
    width = queries.shape[1]
    spans, heads = tokens // SPAN, width // DK
    rows = lax.broadcasted_iota(jnp.int32, (SPAN, SPAN), 0)
    cols = lax.broadcasted_iota(jnp.int32, (SPAN, SPAN), 1)
    inclusive = rows >= cols
    strict = rows > cols
    diagonal = rows == cols
    items = [(span, head) for span in range(spans) for head in range(heads)]


    def cut(block, item):
        span, head = item
        return block[span * SPAN : (span + 1) * SPAN, head * DK : (head + 1) * DK]

    def cut_row(block, item):
        span, head = item
        return block[head : head + 1, span * SPAN : (span + 1) * SPAN]

    def column_of(row):
        return jnp.sum(jnp.where(diagonal, row, 0.0), 1, keepdims=True)

    def row_of(column):
        return jnp.sum(jnp.where(diagonal, column, 0.0), 0, keepdims=True)

    def lower_left(size):
        return (
            (rows // (2 * size) == cols // (2 * size))
            & ((rows // size) % 2 == 1)
            & ((cols // size) % 2 == 0)
        )

    if side == 0:
        gates = refs[0]
        decays, strengths = [
            jnp.where(core == 0, gates[kind, :heads], gates[kind, heads:]) for kind in range(2)
        ]
    else:
        decays, strengths = received_gates(stack, tokens, heads)
    decay_log = jnp.log(decays)
    identity = jnp.where(diagonal, 1.0, 0.0)

    def build(items):
        q = [unit(cut(queries, item)) for item in items]
        k = [unit(cut(keys, item)) for item in items]
        growth_log = [
            jnp.sum(jnp.where(inclusive, cut_row(decay_log, item), 0.0), 1, keepdims=True)
            for item in items
        ]
        strength_row = [cut_row(strengths, item) for item in items]
        inner = [dot_nt(jnp.concatenate([kk, qq], 0), kk) for kk, qq in zip(k, q)]
        ratios = [
            jnp.where(inclusive, jnp.exp(jnp.where(inclusive, log - row_of(log), 0.0)), 0.0)
            for log in growth_log
        ]
        coupling = [
            jnp.where(strict, column_of(row) * ratio * both[:SPAN], 0.0)
            for row, ratio, both in zip(strength_row, ratios, inner)
        ]
        mixing = [ratio * both[SPAN:] for ratio, both in zip(ratios, inner)]
        corner = lower_left(1)
        inverse = [identity - jnp.where(corner, block, 0.0) for block in coupling]
        size = 2
        while size < SPAN:
            corner = lower_left(size)
            narrow = [block.astype(BF16) for block in inverse]
            part = [
                dot(x, jnp.where(corner, a, 0.0).astype(BF16)) for x, a in zip(narrow, coupling)
            ]
            step_back = [dot(y.astype(BF16), x) for y, x in zip(part, narrow)]
            inverse = [x - z for x, z in zip(inverse, step_back)]
            size *= 2
        residual = [identity - x - fine_dot(a, x) for a, x in zip(coupling, inverse)]
        inverse = [x + dot(x.astype(BF16), e.astype(BF16)) for x, e in zip(inverse, residual)]
        scaled = [x * row for x, row in zip(inverse, strength_row)]
        growth = [jnp.exp(log) for log in growth_log]
        grown_keys = [g * kk.astype(F32) for g, kk in zip(growth, k)]
        grown_queries = [g * qq.astype(F32) for g, qq in zip(growth, q)]
        tails = [
            (jnp.exp(log[SPAN - 1 :] - log) * kk.astype(F32)).T for log, kk in zip(growth_log, k)
        ]
        upper = [
            fine_dot(jnp.concatenate([tail, mix], 0), b)
            for tail, mix, b in zip(tails, mixing, scaled)
        ]
        removed = [fine_dot(up, gk) for up, gk in zip(upper, grown_keys)]
        for item, g, up, rem, gq in zip(items, growth, upper, removed, grown_queries):
            span, head = item
            kept = jnp.where(diagonal, g[SPAN - 1 :], 0.0)
            whole = jnp.concatenate([jnp.concatenate([kept, gq], 0) - rem, up], 1)
            high, low = halves(whole.T)
            forth[owner, span, head] = whole.astype(BF16)
            back[owner, span, head] = high
            back_low[owner, span, head] = low

    for start in range(0, len(items), BATCH):
        build(items[start : start + BATCH])


BATCH = 8


def prepare(place, side, tokens, width, stack, others):
    heads = width // DK
    shape = (2, tokens // SPAN, heads, 2 * DK, 2 * DK)
    return kernel_call(
        functools.partial(prepare_kernel, side, tokens),
        "prepare",
        place,
        (stack,) + tuple(others),
        [(shape, BF16)] * 3,
        aliases={2 + index: index for index in range(3)} if side else {},
    )


def owned(place, blocks):
    mine, theirs = blocks
    first = place[0] == 0
    return jnp.where(first, mine, theirs), jnp.where(first, theirs, mine)


def row_block(place, block):
    if isinstance(block, int):
        return block
    chips, core = block
    if core == "same":
        core = place[0]
    elif core == "other":
        core = 1 - place[0]
    return 2 * lax.bitwise_xor(place[1], chips) + core


def columns_of(place, block, width):
    return pl.ds(pl.multiple_of(row_block(place, block) * width, width), width)


def positions_of(owner, tokens):
    return pl.ds(pl.multiple_of(owner * tokens, tokens), tokens)


def load_piece(ref, rows):
    return ref[:rows] if ref.shape[0] < 3 * rows else ref[3 * rows : 4 * rows]


def read_kernel(with_state, blocks, place, mine, theirs, own, stack, back, low, *refs):
    count = len(blocks)
    pieces, refs = refs[:count], refs[count:]
    if with_state:
        (first, *refs) = refs
    (total, kept, given, last, read) = refs
    tokens, width = own.shape[1:]
    spans, heads = back.shape[1:3]
    core = place[0]
    values = owned(place, (own[2], stack[2 * tokens : 3 * tokens]))
    products = product_steps(place, blocks, mine, theirs, pieces, total, None)
    zero = jnp.zeros((DK, DK), F32)
    states = [first[head] if with_state else zero for head in range(heads)]
    for half in range(2):
        for span in range(spans):
            for head in range(heads):
                positions = slice(span * SPAN, (span + 1) * SPAN)
                columns = slice(head * DK, (head + 1) * DK)
                block = values[half][positions, columns].T
                x_high, x_low = halves(states[head])
                left = jnp.concatenate([x_high, block], 1)
                rest = jnp.concatenate([x_low, jnp.zeros_like(block)], 1)
                both = dot(jnp.concatenate([left, rest], 0), back[half, span, head])
                result = both[:DK] + both[DK:] + dot(left, low[half, span, head])
                states[head] = result[:, :DK]
                read[half, positions, columns] = result[:, DK:].T.astype(BF16)
            next(products, None)
    for head in range(heads):
        last[head] = states[head]
    for _ in products:
        pass
    kept[...] = read[core]
    given[...] = read[1 - core]


def paired(blocks):
    return not isinstance(blocks[0], int) and blocks[0][0] == blocks[1][0]


def add_products(place, blocks, mine, theirs, pieces, result, total):
    for _ in product_steps(place, blocks, mine, theirs, pieces, result, total):
        pass


def product_steps(place, blocks, mine, theirs, pieces, result, total):
    tokens = mine.shape[0]
    rows = mine.shape[1] // 8
    core = place[0]
    probe = [load_piece(piece, rows) for piece in pieces]
    for source, owner in ((mine, core), (theirs, 1 - core)):
        positions = positions_of(owner, tokens)
        begin = 0
        part = None if total is None else total[positions, :]
        if paired(blocks):
            chip = lax.bitwise_xor(place[1], blocks[0][0])
            columns = pl.ds(pl.multiple_of(chip * 2 * rows, 2 * rows), 2 * rows)
            product = dot(source[:, columns], jnp.concatenate(owned(place, probe[:2]), 0))
            part = product if part is None else part + product
            begin = 2
            yield
        for block, piece in zip(blocks[begin:], probe[begin:]):
            product = dot(source[:, columns_of(place, block, rows)], piece)
            part = product if part is None else part + product
            yield
        result[positions, :] = part.astype(result.dtype)


def read_values(place, mine, theirs, own, stack, maps, blocks, pieces, entry):
    tokens, width = own.shape[1:]
    heads = width // DK
    extra = () if entry is None else (entry,)
    return kernel_call(
        functools.partial(read_kernel, entry is not None, tuple(blocks)),
        "read_values",
        place,
        (mine, theirs, own, stack, maps[1], maps[2], *pieces, *extra),
        [
            ((2 * tokens, width), F32),
            ((tokens, width), BF16),
            ((tokens, width), BF16),
            ((heads, DK, DK), F32),
        ],
        scratch=[pltpu.VMEM((2, tokens, width), BF16)],
    )


def recur_kernel(weighting, with_state, blocks, chips, lists, place, mine, theirs, total, forth, back, read, *refs):
    count = len(blocks)
    pieces, refs = refs[:count], refs[count:]
    if with_state:
        (first, final, *refs) = refs
    (grads, last, start, *refs) = refs
    width = total.shape[1]
    shares, (sums, up) = refs[: len(lists)], refs[len(lists) :]
    tokens = mine.shape[0]
    spans, heads = forth.shape[1:3]
    add_products(place, blocks, mine, theirs, pieces, sums, total)
    zero = jnp.zeros((DK, DK), F32)
    states = [first[head] if with_state else zero for head in range(heads)]
    steps = [(half, span) for half in range(2) for span in range(spans)]
    for half, span in steps:
        begin = half * tokens + span * SPAN
        for head in range(heads):
            block = sums[begin : begin + SPAN, head * DK : (head + 1) * DK].T.astype(BF16)
            left = jnp.concatenate([states[head].astype(BF16), block], 1)
            result = dot(left, back[half, span, head])
            states[head] = result[:, :DK]
            up[half, span, head] = (weighting * result[:, DK:]).astype(BF16)
    for head in range(heads):
        last[head] = states[head]
    states = [final[head] if with_state else zero for head in range(heads)]
    for half, span in reversed(steps):
        begin = half * tokens + span * SPAN
        for head in range(heads):
            left = jnp.concatenate([states[head].astype(BF16), up[half, span, head]], 1)
            result = dot(left, forth[half, span, head])
            states[head] = result[:, :DK]
            row = begin // width * width + head * DK
            grads[row : row + DK, begin % width : begin % width + SPAN] = result[:, DK:].astype(BF16)
    grads[2 * tokens :, :] = read[...]
    for head in range(heads):
        start[head] = states[head]
    if lists:
        put_products(place, chips, lists, mine, theirs, grads, shares)


def grads_of(grads, owner, tokens):
    width = grads.shape[1]
    block = grads[positions_of(owner, tokens), :]
    return jnp.concatenate([block[i : i + width] for i in range(0, tokens, width)], 1)


def put_products(place, chips, lists, mine, theirs, grads, outs):
    tokens, width = mine.shape
    if chips is None:
        columns = pl.ds(0, width)
    else:
        columns = pl.ds(pl.multiple_of(lax.bitwise_xor(place[1], chips) * 4 * ROWS, 4 * ROWS), 4 * ROWS)
    core = place[0]
    part = dot(grads_of(grads, core, tokens), mine[:, columns])
    part += dot(grads_of(grads, 1 - core, tokens), theirs[:, columns])
    part = part.T
    for out, indices in zip(outs, lists):
        for slot, index in enumerate(indices):
            out[slot] = part[index * ROWS : (index + 1) * ROWS].astype(out.dtype)


def recur(weighting, place, mine, theirs, total, maps, read, blocks, pieces, chips, lists, states):
    tokens = mine.shape[0]
    width = total.shape[1]
    spans, heads = maps[0].shape[1:3]
    extra = () if states is None else states
    return kernel_call(
        functools.partial(
            recur_kernel, weighting, states is not None, tuple(blocks), chips, lists
        ),
        "recur",
        place,
        (mine, theirs, total, maps[0], maps[1], read, *pieces, *extra),
        [((3 * tokens, width), BF16), ((heads, DK, DK), F32), ((heads, DK, DK), F32)]
        + [((len(part), ROWS, width), BF16) for part in lists],
        scratch=[
            pltpu.VMEM((2 * tokens, width), F32),
            pltpu.VMEM((2, spans, heads, DK, SPAN), BF16),
        ],
    )


ROWS = 256


def curvature_kernel(jobs, place, mine, theirs, grads, *outs):
    begin = 0
    for chips, lists in jobs:
        put_products(place, chips, lists, mine, theirs, grads, outs[begin : begin + len(lists)])
        begin += len(lists)


def curvature(place, mine, theirs, grads, jobs, types):
    width = grads.shape[1]
    lengths = [len(part) for chips, lists in jobs for part in lists]
    return kernel_call(
        functools.partial(curvature_kernel, jobs),
        "curvature",
        place,
        (mine, theirs, grads),
        [((length, ROWS, width), kind) for length, kind in zip(lengths, types)],
    )


def keep_kernel(place, mine, theirs, grads, keep_x, keep_y):
    for chips, half, out in ((1, 1, keep_x), (2, 0, keep_y)):
        for block in range(2):
            columns = half_block(place, chips, block, half)
            out[block] = products(place, mine, theirs, grads, columns)


def half_block(place, chips, block, half):
    index = 2 * (2 * lax.bitwise_xor(place[1], chips) + block) + half
    return pl.ds(pl.multiple_of(index * ROWS, ROWS), ROWS)


def products(place, mine, theirs, grads, columns):
    tokens = mine.shape[0]
    core = place[0]
    part = dot(grads_of(grads, core, tokens), mine[:, columns])
    part += dot(grads_of(grads, 1 - core, tokens), theirs[:, columns])
    return part.T


def keep(place, mine, theirs, grads):
    shape = (2, ROWS, grads.shape[1])
    return kernel_call(keep_kernel, "keep", place, (mine, theirs, grads), [(shape, F32)] * 2)


def near_kernel(place, mine, theirs, grads, grads_other, read, near_x, near_y, own, mixed):
    core = place[0]
    tokens, width = read.shape
    join(place, read[...], grads_other[2 * tokens :, :], mixed)
    jobs = (
        (half_block(place, 1, core, 0), near_x),
        (half_block(place, 2, core, 1), near_y),
        (pl.ds(pl.multiple_of((2 * place[1] + core) * 2 * ROWS, 2 * ROWS), 2 * ROWS), own),
    )
    for columns, out in jobs:
        for source, owner in ((grads, core), (grads_other, 1 - core)):
            part = products(place, mine, theirs, source, columns)
            out[:, positions_of(owner, width)] = part.astype(out.dtype)


def near(place, mine, theirs, grads, grads_other, read):
    rows, width = read.shape
    return kernel_call(
        near_kernel,
        "near",
        place,
        (mine, theirs, grads, grads_other, read),
        [
            ((ROWS, 2 * width), BF16),
            ((ROWS, 2 * width), BF16),
            ((2 * ROWS, 2 * width), F32),
            ((rows, 2 * width), BF16),
        ],
    )


def join(place, same, cross, whole):
    width = same.shape[1]
    whole[:, positions_of(place[0], width)] = same
    whole[:, positions_of(1 - place[0], width)] = cross


def relay_kernel(place, far_x, far_y, keep_x, keep_y, after, *outs):
    core = place[0]
    for index, (far, keep) in enumerate(((far_x, keep_y), (far_y, keep_x))):
        for which, owner in enumerate((core, 1 - core)):
            outs[2 * index + which][...] = (keep[owner] + far[owner].astype(F32)).astype(BF16)


def relay(place, far_x, far_y, keep_x, keep_y, after):
    shape = keep_x.shape[1:]
    operands = (far_x, far_y, keep_x, keep_y, after)
    return kernel_call(relay_kernel, "relay", place, operands, [(shape, BF16)] * 4)


def finish_kernel(place, own, near_x, near_y, top_same, low_same, top_cross, low_cross, whole, sums, sems):
    core = place[0]
    width = top_same.shape[1]
    copies = []
    for owner, top, low in ((core, top_same, low_same), (1 - core, top_cross, low_cross)):
        columns = positions_of(owner, width)
        for rows, first, second in ((slice(0, ROWS), near_x, top), (slice(ROWS, 2 * ROWS), near_y, low)):
            part = first[:, columns].astype(F32) + second[...].astype(F32)
            sums[rows, columns] = own[rows, columns] + part
            place_rows = pl.ds(rows.start, ROWS)
            copies.append(
                pltpu.make_async_copy(
                    sums.at[place_rows, columns], whole.at[place_rows, columns], sems.at[len(copies)]
                )
            )
            copies[-1].start()
    for copy in copies:
        copy.wait()


def finish(place, *parts):
    shape = parts[0].shape
    vmem_spec = pl.BlockSpec(memory_space=pltpu.VMEM)
    return pl.pallas_call(
        finish_kernel,
        grid_spec=pltpu.PrefetchScalarGridSpec(
            num_scalar_prefetch=1,
            grid=(),
            in_specs=[vmem_spec] * len(parts),
            out_specs=pl.BlockSpec(memory_space=pltpu.HBM),
            scratch_shapes=[pltpu.VMEM(shape, F32), pltpu.SemaphoreType.DMA((4,))],
        ),
        out_shape=jax.ShapeDtypeStruct(shape, F32),
        compiler_params=pltpu.CompilerParams(vmem_limit_bytes=VMEM_BYTES),
        cost_estimate=cost(0.01),
        name="finish",
    )(place, *(in_vmem(part) for part in parts))


def join_kernel(place, same, cross, whole):
    join(place, same[...], cross[...], whole)


def local(square, dp_size, ctx_size, queries, keys, values, decay, beta, inputs, probe):
    tokens = queries.shape[1]
    width = queries.shape[2] // 2
    weighting = math.sqrt(D) / (dp_size * ctx_size * tokens)
    ctx = lax.axis_index("ctx")
    chip = lax.axis_index("dp")
    core = lax.rem(ctx, 2)
    groups = ctx_size // 2
    partner = [(index, index ^ 1) for index in range(ctx_size)]
    mine = inputs[0]
    place = jnp.stack([core, chip])

    def swap(block):
        return lax.ppermute(block, "ctx", partner)

    def send(block, chips, cores):
        pairs = [
            (2 * index + which, 2 * (index ^ chips) + (which ^ cores))
            for index in range(dp_size)
            for which in range(2)
        ]
        return lax.ppermute(block, GROUP, pairs)

    def part(block, index):
        return lax.dynamic_slice_in_dim(block, index * width, width, 1)

    kept, given, own, stack, gates = pack(place, square, queries, keys, values, decay, beta, probe)
    if square:
        stack, mine = lax.optimization_barrier((stack, mine))
        stack = swap(stack)
        theirs = swap(mine)
        x_one = send(kept, 1, 0)
        y_one = send(given, 2, 1)
        x_two = send(given, 1, 1)
        maps = prepare(place, 0, tokens, width, own, (gates,))
        late, *maps = lax.optimization_barrier((kept, *maps))
        y_two = send(late, 2, 0)
        x_one, y_one, *maps = lax.optimization_barrier((x_one, y_one, *maps))
        far_one = send(x_one, 2, 0)
        far_two = send(y_one, 1, 0)
        maps = prepare(place, 1, tokens, width, stack, maps)
        pieces = [kept, stack, x_one, y_one, x_two, y_two, far_one, far_two]
        places = [
            (0, "same"),
            (0, "other"),
            (1, "same"),
            (2, "other"),
            (1, "other"),
            (2, "same"),
            (3, "same"),
            (3, "other"),
        ]
    else:
        stack = swap(stack)
        theirs = swap(mine)
        maps = prepare(place, 0, tokens, width, own, (gates,))
        maps = prepare(place, 1, tokens, width, stack, maps)
        gathered = part(lax.all_gather(probe, GROUP, axis=0, tiled=True), core)
        places = list(range(8))
        rows = D // len(places)
        pieces = [gathered[index * rows : (index + 1) * rows] for index in places]
    def shift(block, by):
        pairs = [
            (index, index + 2 * by)
            for index in range(ctx_size)
            if 0 <= index + 2 * by < ctx_size
        ]
        return lax.ppermute(block, "ctx", pairs)

    entry = None
    if groups > 1:
        entry = jnp.zeros((width // DK, DK, DK), F32)
    read = functools.partial(
        read_values,
        place,
        mine,
        theirs,
        own,
        stack,
        maps,
        places[:6],
        pieces[:6],
    )
    for _ in range(groups - 1):
        entry = shift(read(entry)[3], 1)
    total, read_kept, read_given, unused = read(entry)
    lists = ((0, 2), (1, 3)) if square else ()
    run = functools.partial(
        recur,
        weighting,
        place,
        mine,
        theirs,
        total,
        maps,
        read_given,
        places[6:],
        pieces[6:],
        3,
        lists,
    )
    states = None
    if groups > 1:
        states = (jnp.zeros((width // DK, DK, DK), F32),) * 2
        for _ in range(groups - 1):
            states = (shift(run(states)[1], 1), states[1])
        for _ in range(groups - 1):
            states = (states[0], shift(run(states)[2], -1))
    grads, unused, unused, *shares = run(states)
    build = functools.partial(curvature, place, mine, theirs, grads)
    if not square:
        everything = build(((None, (tuple(range(D // ROWS)),)),), [F32])[0]
        flat = everything.reshape(D, width)
        zero = jnp.zeros_like(flat)
        both = jnp.where(
            core == 0, jnp.concatenate([flat, zero], 1), jnp.concatenate([zero, flat], 1)
        )
        read_swapped = swap(read_given)
        mixed = kernel_call(
            join_kernel, "join", place, (read_kept, read_swapped), [((tokens, 2 * width), BF16)]
        )[0]
        return mixed[None], lax.psum_scatter(both, GROUP, scatter_dimension=0, tiled=True)

    far_x = send(shares[0], 1, 0)
    far_y = send(shares[1], 2, 0)
    grads_other = swap(grads)
    keep_x, keep_y = keep(place, mine, theirs, grads)
    near_x, near_y, rest, mixed = near(place, mine, theirs, grads, grads_other, read_kept)
    after = near_x
    near_x = send(near_x, 1, 0)
    near_y = send(near_y, 2, 0)
    top_same, top_cross, low_same, low_cross = relay(place, far_x, far_y, keep_x, keep_y, after)
    top_same = send(top_same, 2, 0)
    low_same = send(low_same, 1, 0)
    near_x, low_cross = lax.optimization_barrier((near_x, low_cross))
    top_cross = send(top_cross, 2, 1)
    low_cross = send(low_cross, 1, 1)
    result = finish(place, rest, near_x, near_y, top_same, low_same, top_cross, low_cross)
    return mixed[None], result


def solution(mesh):
    dp_size, ctx_size = mesh.shape["dp"], mesh.shape["ctx"]
    square = dp_size == 4 and ctx_size == 2
    return jax.shard_map(
        functools.partial(local, square, dp_size, ctx_size),
        mesh=mesh,
        in_specs=(
            P("dp", "ctx", "head"),
            P("dp", "ctx", "head"),
            P("dp", "ctx", "head"),
            P("dp", "head", "ctx"),
            P("dp", "head", "ctx"),
            P("dp", "ctx", None),
            P(("dp", "ctx"), "head"),
        ),
        out_specs=(P("dp", "ctx", "head"), P(("dp", "ctx"), "head")),
        check_vma=False,
    )
```
